256 devices in a mesh: group: 8 (over z), shard: 32 (over y, x, core).
Axes of the slice: x: 4, y: 4, z: 8, core: 2. Of those that a mesh axis runs over, the one named last changes fastest.
Arguments:
- queries: bfloat16 [4096, 32, 128], P(('group', 'shard')), parts along dimension 0, may hold values from -6 to 6
- passages: bfloat16 [4096, 180, 128], P('shard'), may hold values from -6 to 6
- lengths: int32 [4096], P('shard'), may hold values from 8 to 180
- candidates: int32 [4096, 64], P(('group', 'shard')), parts along dimension 0, may hold values from 0 to 4095, as said below
Outputs:
- scores: float32 [4096, 64], P(('group', 'shard')), parts along dimension 0
The draws below stay inside these ranges and needn't reach their ends.
There are 8 independent parts, one for each index of `group`. The reference program is written for one: setup_inputs(seed, part) draws one part's arguments, and reference() takes and returns one part's arrays. A program takes and returns all parts, laid end to end along the dimension named above; an argument that names none is the same for every part. Nothing has to cross between parts.
Inputs may be any that keep to these rules, and one draw needn't show every extreme that they name: Candidate ids of one query are distinct. For the queries of one device (aligned blocks of 16 rows) at most 96 candidates fall in the block of 128 passages of any one device, and exactly 96 fall in one such block.
All inputs are finite; a program needn't handle non-finite values.
Results may differ from the reference program's by a relative error of at most 0.0003.
Values may be sent and summed in bfloat16 or wider, within the bound.
A program may use at most 128 MiB of HBM per device.

```python
import jax
import jax.numpy as jnp
from jax import lax

DIM = 128
QTOK = 32
PLEN = 180
PASS_DEV = 128
QPD = 16
CAND = 64
CAP = 96
PASSAGES = 4096
QUERIES = 512
N_SHARD = 32


def draw_candidates(key, part):
    key = jax.random.fold_in(key, 7)
    hot_key, block_key, shuffle_key = jax.random.split(key, 3)
    hot_owner = jax.random.randint(hot_key, (), 0, N_SHARD)
    total_slots = QPD * CAND
    remainder = total_slots - CAP
    dest_ids = jnp.arange(N_SHARD, dtype=jnp.int32)

    def one_block(block_seed):
        weight_key, extra_key, order_key = jax.random.split(block_seed, 3)
        weights = jax.random.randint(weight_key, (N_SHARD,), 2, 4)
        weights = jnp.where(dest_ids == hot_owner, 0, weights)
        counts = remainder * weights // jnp.sum(weights)
        extra_owner = (hot_owner + 1 + jax.random.randint(extra_key, (), 0, N_SHARD - 1)) % N_SHARD
        counts = counts + jnp.where(dest_ids == extra_owner, remainder - jnp.sum(counts), 0)
        counts = jnp.where(dest_ids == hot_owner, CAP, counts)
        ends = jnp.cumsum(counts)
        starts = ends - counts
        flat_slots = jnp.arange(total_slots, dtype=jnp.int32)
        owner_of = jnp.sum((flat_slots[:, None] >= ends[None, :]).astype(jnp.int32), axis=1)
        within = flat_slots - starts[owner_of]
        orderings = jax.vmap(lambda subkey: jax.random.permutation(subkey, PASS_DEV))(jax.random.split(order_key, N_SHARD * QPD))
        orderings = orderings.reshape(N_SHARD, QPD, PASS_DEV)
        local_pick = orderings[owner_of, flat_slots % QPD, within // QPD]
        cand_ids = owner_of * PASS_DEV + local_pick
        return cand_ids.reshape(CAND, QPD).T
    blocks = jax.vmap(one_block)(jax.random.split(block_key, N_SHARD))
    cand_ids = blocks.reshape(N_SHARD * QPD, CAND)
    row_total = N_SHARD * QPD
    shuffles = jax.vmap(lambda subkey: jax.random.permutation(subkey, CAND))(jax.random.split(shuffle_key, row_total))
    return jnp.take_along_axis(cand_ids, shuffles, axis=1).astype(jnp.int32)


def touch_ends(result, rng, least, largest):
    longest = result.shape.index(max(result.shape))
    spots = []
    for shift in (0, 1):
        where = [jax.random.randint(jax.random.fold_in(rng, axis), (), 0, length) for axis, length in enumerate(result.shape)]
        where[longest] = (where[longest] + shift) % result.shape[longest]
        spots.append(tuple(where))
    return result.at[spots[0]].set(least).at[spots[1]].set(largest)


def block_scale(stream_key, dims, pieces, least, high):
    gain = 1.0
    for position, parts in pieces:
        heights = jax.random.uniform(jax.random.fold_in(jax.random.fold_in(stream_key, 6), position), (parts,), jnp.float32, least / len(pieces), high / len(pieces))
        gain = gain * jnp.repeat(jnp.exp(heights), dims[position] // parts).reshape((-1,) + (1,) * (len(dims) - 1 - position))
    return gain


def scatter_about(key, shape, scale, reach, pieces=(), held_as=jnp.bfloat16):
    array = scale * jax.random.normal(key, shape, jnp.float32)
    if pieces:
        array = array * block_scale(key, shape, pieces, -0.22, 0.18)
    return jnp.clip(array, -reach, reach).astype(held_as)


def setup_inputs(seed: int = 0, part: int = 0) -> dict:
    splits = jax.random.split(jax.random.key(seed), 5)
    part_keys = jax.random.split(jax.random.fold_in(splits[4], part), 5)
    return {
        "queries": scatter_about(part_keys[0], (QUERIES, QTOK, DIM), 1.0, 6.0, ((0, 32),)),
        "passages": scatter_about(splits[1], (PASSAGES, PLEN, DIM), 1.0, 6.0, ((0, 32),)),
        "lengths": touch_ends(jax.random.randint(splits[2], (PASSAGES,), 8, PLEN + 1), jax.random.fold_in(splits[2], 1), 8, PLEN).astype(jnp.int32),
        "candidates": draw_candidates(jax.random.fold_in(jax.random.fold_in(splits[4], part), 71), part),
    }


def reference(queries, passages, lengths, candidates):
    positions = jnp.arange(PLEN, dtype=jnp.int32)

    def one_query(block_args):
        query_tokens, cand_ids = block_args
        chosen = passages[cand_ids].astype(jnp.float32)
        similar = jnp.einsum("id,ctd->cit", query_tokens.astype(jnp.float32), chosen)
        inside = positions[None, None, :] < lengths[cand_ids][:, None, None]
        best_match = jnp.max(jnp.where(inside, similar, jnp.float32(-1e30)), axis=2)
        return jnp.mean(best_match, axis=1)

    return lax.map(one_query, (queries, candidates))
```

```python
import functools
import jax, jax.numpy as jnp
from jax import lax
from jax.experimental import pallas as pl
from jax.experimental.pallas import tpu as pltpu
from jax.sharding import PartitionSpec as P

F32, BF16, I32 = jnp.float32, jnp.bfloat16, jnp.int32
UNROLL = 16
PASS_DEV = 128
SLOTS = 512
BOUNDS = (48, 96, 144)


def nt(a, b):
    return lax.dot_general(a, b, (((1,), (1,)), ((), ())), preferred_element_type=F32)


def score_kernel(len_smem, qall, table, len_row, passages, out, pbuf, ranks, acc, lists, lists_smem, psem, lsem):
    pcount, plen, dim = passages.shape
    qcount, qtok, _ = qall.shape
    chunk = pcount // 4
    loads = [
        pltpu.make_async_copy(passages.at[pl.ds(i * chunk, chunk)], pbuf.at[pl.ds(i * chunk, chunk)], psem.at[i])
        for i in range(4)
    ]
    for load in loads:
        load.start()
    hit = table[...]
    row = lax.broadcasted_iota(I32, (qcount, qcount), 0)
    col = lax.broadcasted_iota(I32, (qcount, qcount), 1)
    before = jnp.where(col < row, 1.0, 0.0).astype(BF16)
    rank = jnp.dot(before, hit, preferred_element_type=F32)
    count = lax.dot_general(hit, jnp.ones((qcount, pcount), BF16), (((0,), (0,)), ((), ())), preferred_element_type=F32)
    blocks = jnp.floor((count + 7.0) * 0.125)
    lens = len_row[...].astype(F32)

    def class_of(lens):
        return sum(jnp.where(lens > float(bound), 1.0, 0.0) for bound in BOUNDS)

    lens_down = jnp.transpose(jnp.broadcast_to(lens, (pcount, pcount)))
    class_down = class_of(lens_down)
    p_down = lax.broadcasted_iota(I32, (pcount, pcount), 0).astype(F32)
    p_across = lax.broadcasted_iota(I32, (pcount, pcount), 1).astype(F32)
    ahead = jnp.where(class_of(lens) * pcount + p_across < class_down * pcount + p_down, 1.0, 0.0).astype(BF16)
    base = jnp.dot(ahead, blocks.astype(BF16), preferred_element_type=F32)
    wide = SLOTS // pcount
    base_w = jnp.concatenate([base] * wide, axis=1)
    blocks_w = jnp.concatenate([blocks] * wide, axis=1)
    slot = lax.broadcasted_iota(I32, (pcount, SLOTS), 1).astype(F32)
    owner = jnp.where(jnp.logical_and(slot >= base_w, slot < base_w + blocks_w), 1.0, 0.0)
    owner_p = jnp.sum(owner * lax.broadcasted_iota(I32, (pcount, SLOTS), 0).astype(F32), axis=0, keepdims=True)
    owner_base = jnp.sum(owner * base_w, axis=0, keepdims=True)
    block_of = jnp.floor(rank * 0.125)
    place = rank - 8.0 * block_of
    keyed = jnp.concatenate([jnp.where(hit > 0, block_of, 128.0).astype(BF16), place.astype(BF16)], axis=1)
    owner_b = owner.astype(BF16)
    weights = jnp.concatenate([(owner * 8.0).astype(BF16), owner_b], axis=0)
    seen = jnp.dot(keyed, weights, preferred_element_type=F32)
    seen = seen - 8.0 * (slot[:1] - owner_base)
    ranks[...] = seen
    q_down = lax.broadcasted_iota(I32, (qcount, SLOTS), 0).astype(F32)
    for k in range(8):
        ids = jnp.sum(jnp.where(seen == float(k), q_down, 0.0), axis=0, keepdims=True)
        lists[pl.ds(k, 1), :] = jnp.clip(ids.astype(I32), 0, qcount - 1)
    lists[pl.ds(8, 1), :] = jnp.clip(owner_p.astype(I32), 0, pcount - 1)
    for c in range(len(BOUNDS) + 1):
        ends = jnp.sum(jnp.where(class_down <= float(c), blocks_w[:, :pcount], 0.0), axis=0, keepdims=True)
        lists[pl.ds(9 + c, 1), :] = jnp.concatenate([ends] * wide, axis=1).astype(I32)
    move = pltpu.make_async_copy(lists, lists_smem, lsem)
    move.start()
    move.wait()
    for load in loads:
        load.wait()

    start = 0
    for c, rows in enumerate(BOUNDS + (plen,)):
        end = lists_smem[9 + c, 0]
        down = lax.broadcasted_iota(I32, (rows, 1), 0)

        def step(i, _, start=start, rows=rows, down=down):
            for u in range(UNROLL):
                b = start + i * UNROLL + u
                p = lists_smem[8, b]
                tokens = jnp.concatenate([qall[lists_smem[k, b]] for k in range(8)], axis=0)
                similar = nt(pbuf[p, :rows], tokens)
                similar = jnp.where(down < len_smem[p], similar, -1e30)
                acc[pl.ds(b, 1), :] = jnp.max(similar, axis=0, keepdims=True)
            return 0

        lax.fori_loop(0, (end - start + UNROLL - 1) // UNROLL, step, 0)
        start = end
    best = acc[:SLOTS]
    token = lax.broadcasted_iota(I32, (8, 8 * qtok), 1)
    mean = jnp.where(token // qtok == lax.broadcasted_iota(I32, (8, 8 * qtok), 0), 1.0 / qtok, 0.0).astype(BF16)
    high = best.astype(BF16)
    scores = nt(mean, high) + nt(mean, (best - high.astype(F32)).astype(BF16))
    seen = ranks[...]
    dense = sum(jnp.where(seen == float(k), scores[k : k + 1], 0.0) for k in range(8))
    high = dense.astype(BF16)
    out[...] = nt(high, owner_b) + nt((dense - high.astype(F32)).astype(BF16), owner_b)


def score(queries, table, lengths, passages):
    pcount, plen, dim = passages.shape
    qcount, qtok, _ = queries.shape
    smem, vmem = pl.BlockSpec(memory_space=pltpu.SMEM), pl.BlockSpec(memory_space=pltpu.VMEM)
    return pl.pallas_call(
        score_kernel,
        out_shape=jax.ShapeDtypeStruct((qcount, pcount), F32),
        in_specs=[smem, vmem, vmem, vmem, pl.BlockSpec(memory_space=pl.ANY)],
        out_specs=vmem,
        scratch_shapes=[
            pltpu.VMEM((pcount, plen, dim), BF16),
            pltpu.VMEM((qcount, SLOTS), F32),
            pltpu.VMEM((SLOTS + 2 * UNROLL, 8 * qtok), F32),
            pltpu.VMEM((16, SLOTS), I32),
            pltpu.SMEM((16, SLOTS), I32),
            pltpu.SemaphoreType.DMA((4,)),
            pltpu.SemaphoreType.DMA,
        ],
        compiler_params=pltpu.CompilerParams(vmem_limit_bytes=48 << 20),
        name="score",
    )(lengths, queries, table, lengths.reshape(1, -1), passages)


SIDE = 4
MESH = pl.DeviceIdType.MESH


def meet(me, count):
    barrier = pltpu.get_barrier_semaphore()

    def tell(k, _):
        peer = lax.rem(me + k, count)
        pl.semaphore_signal(barrier, inc=1, device_id={"shard": peer}, device_id_type=MESH)
        return 0

    lax.fori_loop(1, count, tell, 0)
    return lambda: pl.semaphore_wait(barrier, count - 1)


def gather_kernel(
    count, q_ref, cand_ref, qall, table, wide, slabs, send, recv, near_send, near_recv, slab_send, slab_recv, own_sem
):
    me = lax.axis_index("shard")
    core, x, y = me % 2, (me // 2) % SIDE, me // (2 * SIDE)
    block, ids = cand_ref.shape
    part = block // 2
    sibling = me + 1 - 2 * core
    arrive = meet(me, count)
    own_copy = pltpu.make_async_copy(q_ref, qall.at[pl.ds(me * block, block)], own_sem)
    own_copy.start()

    cand = cand_ref[...]
    across = lax.broadcasted_iota(jnp.int32, (ids, PASS_DEV), 1)
    down = lax.broadcasted_iota(jnp.int32, (count, ids), 0)
    local_down = jnp.transpose((cand % PASS_DEV).astype(F32)).astype(I32)
    for q in range(block):
        by_owner = jnp.where(cand[q : q + 1] // PASS_DEV == down, 1.0, 0.0).astype(BF16)
        by_local = jnp.where(local_down[:, q : q + 1] == across, 1.0, 0.0).astype(BF16)
        wide[:, q, :] = jnp.dot(by_owner, by_local, preferred_element_type=F32)
    slabs[...] = wide[...].astype(BF16)
    arrive()

    def slab_copy(k):
        peer = lax.rem(me + k, count)
        return pltpu.make_async_remote_copy(
            src_ref=slabs.at[peer],
            dst_ref=table.at[pl.ds(me * block, block)],
            send_sem=slab_send.at[k],
            recv_sem=slab_recv.at[k],
            device_id={"shard": peer},
            device_id_type=MESH,
        )

    def each(action):
        def go(k, _):
            action(slab_copy(k))
            return 0

        lax.fori_loop(1, count, go, 0)

    each(lambda copy: copy.start())
    table[pl.ds(me * block, block), :] = slabs[me]

    def device(half, first, second):
        px, py = (first, second) if half == 0 else (second, first)
        return (lax.rem(py + SIDE, SIDE) * SIDE + lax.rem(px + SIDE, SIDE)) * 2 + core

    pos = ((x, y), (y, x))
    waits = []

    def push(half, index, first, second, piece, target, own=False):
        a, b = pos[half]
        offset = half * part + piece[0]
        start = device(half, a + first, b + second) * block + offset
        dst = qall.at[pl.ds(start, piece[1])]
        near = target is None
        copy = pltpu.make_async_remote_copy(
            src_ref=q_ref.at[pl.ds(offset, piece[1])] if own else dst,
            dst_ref=dst,
            send_sem=(near_send if near else send).at[half, index],
            recv_sem=(near_recv if near else recv).at[half, index],
            device_id={"shard": sibling if near else device(half, a + target[0], b + target[1])},
            device_id_type=MESH,
        )
        copy.start()
        waits.append(copy.wait_send)
        if near:
            waits.append(copy.wait_recv)
        return copy

    full, low, high = (0, part), (0, part // 2), (part // 2, part // 2)
    halves = (0, 1)
    a = [push(h, 0, 0, 0, full, (1, 0), True) for h in halves]
    b = [push(h, 1, 0, 0, full, (-1, 0), True) for h in halves]
    up, down_, around = {}, {}, {}

    def second_axis(h, j, offset):
        up[h, j] = push(h, 4 + 4 * j, offset, 0, full, (0, 1), j == 0)
        down_[h, j] = push(h, 5 + 4 * j, offset, 0, full, (0, -1), j == 0)

    for h in halves:
        second_axis(h, 0, 0)
    for h in halves:
        push(h, 0, 0, 0, full, None, True)
    c, d = [], []
    for h in halves:
        a[h].wait_recv()
        c.append(push(h, 2, -1, 0, low, (1, 0)))
        second_axis(h, 1, -1)
        b[h].wait_recv()
        d.append(push(h, 3, 1, 0, high, (-1, 0)))
        second_axis(h, 2, 1)
    for h in halves:
        push(h, 1, -1, 0, full, None)
        push(h, 2, 1, 0, full, None)
    for h in halves:
        c[h].wait_recv()
        d[h].wait_recv()
        second_axis(h, 3, 2)
    for h in halves:
        push(h, 3, 2, 0, full, None)
    shift = (0, -1, 1, 2)
    last = []
    for j in range(4):
        for h in halves:
            up[h, j].wait_recv()
            last.append(push(h, 6 + 4 * j, shift[j], -1, low, (0, 1)))
            push(h, 4 + 4 * j, shift[j], -1, full, None)
            down_[h, j].wait_recv()
            last.append(push(h, 7 + 4 * j, shift[j], 1, high, (0, -1)))
            push(h, 5 + 4 * j, shift[j], 1, full, None)
    for i, (j, h) in enumerate((j, h) for j in range(4) for h in halves):
        last[2 * i].wait_recv()
        last[2 * i + 1].wait_recv()
        push(h, 6 + 4 * j, shift[j], 2, full, None)
    for wait in waits:
        wait()
    each(lambda copy: copy.wait())
    own_copy.wait()


def gather(queries, candidates, count):
    block, qtok, dim = queries.shape
    vmem = pl.BlockSpec(memory_space=pltpu.VMEM)
    dma = pltpu.SemaphoreType.DMA
    return pl.pallas_call(
        functools.partial(gather_kernel, count),
        out_shape=(
            jax.ShapeDtypeStruct((count * block, qtok, dim), BF16),
            jax.ShapeDtypeStruct((count * block, PASS_DEV), BF16),
        ),
        in_specs=[vmem, vmem],
        out_specs=(vmem, vmem),
        scratch_shapes=[
            pltpu.VMEM((count, block, PASS_DEV), F32),
            pltpu.VMEM((count, block, PASS_DEV), BF16),
            dma((2, 20)),
            dma((2, 20)),
            dma((2, 20)),
            dma((2, 20)),
            dma((count,)),
            dma((count,)),
            dma,
        ],
        compiler_params=pltpu.CompilerParams(collective_id=0, has_side_effects=True, vmem_limit_bytes=24 << 20),
        name="gather",
    )(queries, candidates)


def return_kernel(count, dense, cand_ref, out, slabs, send, recv):
    me = lax.axis_index("shard")
    block, ids = cand_ref.shape
    meet(me, count)()

    def slab_copy(k):
        peer = lax.rem(me + k, count)
        return pltpu.make_async_remote_copy(
            src_ref=dense.at[pl.ds(peer * block, block)],
            dst_ref=slabs.at[me],
            send_sem=send.at[k],
            recv_sem=recv.at[k],
            device_id={"shard": peer},
            device_id_type=MESH,
        )

    def each(action):
        def go(k, _):
            action(slab_copy(k))
            return 0

        lax.fori_loop(1, count, go, 0)

    each(lambda copy: copy.start())
    slabs[me] = dense[pl.ds(me * block, block), :]
    cand = cand_ref[...]
    local = cand % PASS_DEV
    local = jnp.concatenate([local] * (PASS_DEV // ids), axis=1)
    owner = cand // PASS_DEV
    each(lambda copy: copy.wait())
    total = jnp.zeros((block, ids), F32)
    for o in range(count):
        found = jnp.take_along_axis(slabs[o], local, axis=1)[:, :ids]
        total = jnp.where(owner == o, found, total)
    out[...] = total


def give_back(dense, candidates, count):
    block, ids = candidates.shape
    vmem = pl.BlockSpec(memory_space=pltpu.VMEM)
    dma = pltpu.SemaphoreType.DMA
    return pl.pallas_call(
        functools.partial(return_kernel, count),
        out_shape=jax.ShapeDtypeStruct((block, ids), F32),
        in_specs=[vmem, vmem],
        out_specs=vmem,
        scratch_shapes=[pltpu.VMEM((count, block, PASS_DEV), F32), dma((count,)), dma((count,))],
        compiler_params=pltpu.CompilerParams(collective_id=1, has_side_effects=True),
        name="give_back",
    )(dense, candidates)


def shards(queries, passages, lengths, candidates):
    count = lax.axis_size("shard")
    every, table = gather(queries, candidates, count)
    dense = score(every, table, lengths, passages)
    return give_back(dense, candidates, count)


def solution(mesh):
    in_specs = (
        P(("group", "shard"), None, None),
        P("shard", None, None),
        P("shard"),
        P(("group", "shard"), None),
    )
    out_specs = P(("group", "shard"), None)
    return jax.shard_map(shards, mesh=mesh, in_specs=in_specs, out_specs=out_specs, check_vma=False)
```

```python
import functools

import jax
import jax.numpy as jnp
from jax import lax
from jax.experimental import pallas as pl
from jax.experimental.pallas import tpu as pltpu
from jax.sharding import PartitionSpec as P

F32, BF16, I32 = jnp.float32, jnp.bfloat16, jnp.int32
MESH = pl.DeviceIdType.MESH
SIDE = 4
LANES = 128
UNROLL = 16
BOUNDS = (48, 96, 144)


def nt(a, b):
    return lax.dot_general(a, b, (((1,), (1,)), ((), ())), preferred_element_type=F32)


def place_of(cand, pass_dev):
    half = pass_dev // 2
    within = cand % pass_dev
    owner = cand // (2 * pass_dev) * 2 + within // half
    return owner, cand // pass_dev % 2 * half + within % half


def meet(me, count):
    barrier = pltpu.get_barrier_semaphore()

    def tell(k, _):
        pl.semaphore_signal(barrier, inc=1, device_id={"shard": (me + k) % count}, device_id_type=MESH)
        return 0

    lax.fori_loop(1, count, tell, 0)
    return lambda: pl.semaphore_wait(barrier, count - 1)


def gather_kernel(
    count,
    q_ref,
    cand_ref,
    pass_ref,
    len_ref,
    qall,
    pbuf,
    lists,
    ranks,
    owners,
    cand_buf,
    lens_near,
    lens_far,
    wide,
    slabs,
    table,
    stage,
    send,
    recv,
    near_send,
    near_recv,
    slab_send,
    slab_recv,
    own_sem,
    pass_send,
    pass_recv,
):
    me = lax.axis_index("shard")
    core, x, y = me % 2, (me // 2) % SIDE, me // (2 * SIDE)
    block, ids = cand_ref.shape
    plen, pcount, dim = pass_ref.shape
    qcount = qall.shape[0]
    tiles = ranks.shape[0]
    slots = tiles * LANES
    part, phalf = block // 2, pcount // 2
    sibling = me + 1 - 2 * core
    arrive = meet(me, count)
    own_half = pl.ds(pl.multiple_of(core * phalf, phalf), phalf)
    other_half = pl.ds(pl.multiple_of((1 - core) * phalf, phalf), phalf)
    fetch_cand = pltpu.make_async_copy(cand_ref, cand_buf, own_sem.at[0])
    fetch_pass = pltpu.make_async_copy(pass_ref.at[:, own_half, :], stage.at[:, own_half, :], own_sem.at[1])
    fetch_q = pltpu.make_async_copy(q_ref, qall.at[pl.ds(me * block, block)], own_sem.at[2])
    fetch_len = pltpu.make_async_copy(len_ref, lens_near, own_sem.at[3])
    for fetch in (fetch_cand, fetch_pass, fetch_q, fetch_len):
        fetch.start()

    fetch_cand.wait()
    owner, local = place_of(cand_buf[...], pcount)
    across = lax.broadcasted_iota(I32, (ids, pcount), 1)
    down = lax.broadcasted_iota(I32, (count, ids), 0)
    local_down = jnp.transpose(local.astype(F32)).astype(I32)
    for q in range(block):
        by_owner = jnp.where(owner[q : q + 1] == down, 1.0, 0.0).astype(BF16)
        by_local = jnp.where(local_down[:, q : q + 1] == across, 1.0, 0.0).astype(BF16)
        wide[:, q, :] = jnp.dot(by_owner, by_local, preferred_element_type=F32)
    slabs[...] = wide[...].astype(BF16)
    arrive()

    def device(half, first, second):
        px, py = (first, second) if half == 0 else (second, first)
        return ((py + SIDE) % SIDE * SIDE + (px + SIDE) % SIDE) * 2 + core

    pos = ((x, y), (y, x))
    waits = []

    def push(half, index, first, second, piece, target, own=False):
        a, b = pos[half]
        offset = half * part + piece[0]
        start = device(half, a + first, b + second) * block + offset
        dst = qall.at[pl.ds(start, piece[1])]
        near = target is None
        copy = pltpu.make_async_remote_copy(
            src_ref=q_ref.at[pl.ds(offset, piece[1])] if own else dst,
            dst_ref=dst,
            send_sem=(near_send if near else send).at[half, index],
            recv_sem=(near_recv if near else recv).at[half, index],
            device_id={"shard": sibling if near else device(half, a + target[0], b + target[1])},
            device_id_type=MESH,
        )
        copy.start()
        waits.append(copy.wait_send)
        if near:
            waits.append(copy.wait_recv)
        return copy

    def slab_copy(k):
        peer = (me + k) % count
        return pltpu.make_async_remote_copy(
            src_ref=slabs.at[peer],
            dst_ref=table.at[pl.ds(pl.multiple_of(me * block, block), block)],
            send_sem=slab_send.at[k],
            recv_sem=slab_recv.at[k],
            device_id={"shard": peer},
            device_id_type=MESH,
        )

    def each(action):
        def go(k, _):
            action(slab_copy(k))
            return 0

        lax.fori_loop(1, count, go, 0)

    full, low, high = (0, part), (0, part // 2), (part // 2, part // 2)
    halves = (0, 1)
    a = [push(h, 0, 0, 0, full, (1, 0), True) for h in halves]
    b = [push(h, 1, 0, 0, full, (-1, 0), True) for h in halves]
    up, down_ = {}, {}

    def second_axis(h, j, offset):
        up[h, j] = push(h, 4 + 4 * j, offset, 0, full, (0, 1), j == 0)
        down_[h, j] = push(h, 5 + 4 * j, offset, 0, full, (0, -1), j == 0)

    for h in halves:
        second_axis(h, 0, 0)
    each(lambda copy: copy.start())

    def to_sibling(src, dst, index):
        copy = pltpu.make_async_remote_copy(
            src_ref=src,
            dst_ref=dst,
            send_sem=pass_send.at[index],
            recv_sem=pass_recv.at[index],
            device_id={"shard": sibling},
            device_id_type=MESH,
        )
        copy.start()
        return copy

    give_pass = to_sibling(pass_ref.at[:, other_half, :], stage.at[:, own_half, :], 0)
    give_len = to_sibling(len_ref, lens_far, 1)
    for h in halves:
        push(h, 0, 0, 0, full, None, True)
    table[pl.ds(pl.multiple_of(me * block, block), block), :] = slabs[me]

    def relay(which):
        first = which * phalf

        def go(i, _):
            p = pl.multiple_of(first + i % (phalf // 16) * 16, 16)
            t = pl.multiple_of(i // (phalf // 16) * 16, 16)
            pbuf[pl.ds(p, 16), pl.ds(t, 16), :] = jnp.swapaxes(stage[pl.ds(t, 16), pl.ds(p, 16), :], 0, 1)
            return 0

        lax.fori_loop(0, plen // 16 * (phalf // 16), go, 0)
        rest = plen // 16 * 16
        if rest < plen:
            for i in range(phalf // 16):
                p = pl.multiple_of(first + i * 16, 16)
                pbuf[pl.ds(p, 16), rest:plen, :] = jnp.swapaxes(stage[rest:plen, pl.ds(p, 16), :], 0, 1)

    fetch_pass.wait()
    relay(core)

    shift = (0, -1, 1, 2)
    last = []

    def second_forward(j):
        for h in halves:
            up[h, j].wait_recv()
            last.append(push(h, 6 + 4 * j, shift[j], -1, low, (0, 1)))
            down_[h, j].wait_recv()
            last.append(push(h, 7 + 4 * j, shift[j], 1, high, (0, -1)))

    def second_near(j):
        for h in halves:
            push(h, 4 + 4 * j, shift[j], -1, full, None)
            push(h, 5 + 4 * j, shift[j], 1, full, None)

    c, d = [], []
    for h in halves:
        a[h].wait_recv()
        c.append(push(h, 2, -1, 0, low, (1, 0)))
        second_axis(h, 1, -1)
        b[h].wait_recv()
        d.append(push(h, 3, 1, 0, high, (-1, 0)))
        second_axis(h, 2, 1)
    second_forward(0)
    for h in halves:
        push(h, 1, -1, 0, full, None)
        push(h, 2, 1, 0, full, None)
    second_near(0)

    each(lambda copy: copy.wait_recv())
    hit = table[...]
    row = lax.broadcasted_iota(I32, (qcount, qcount), 0)
    col = lax.broadcasted_iota(I32, (qcount, qcount), 1)
    rank = jnp.dot(jnp.where(col < row, 1.0, 0.0).astype(BF16), hit, preferred_element_type=F32)
    number = lax.dot_general(hit, jnp.ones((qcount, pcount), BF16), (((0,), (0,)), ((), ())), preferred_element_type=F32)
    blocks = jnp.floor((number + 7.0) * 0.125)
    fetch_len.wait()
    give_len.wait_recv()
    mine, theirs = lens_near[...].astype(F32), lens_far[...].astype(F32)
    even, odd = jnp.where(core == 0, mine, theirs), jnp.where(core == 0, theirs, mine)
    lens = jnp.where(
        core == 0,
        jnp.concatenate([even[:, :phalf], odd[:, :phalf]], axis=1),
        jnp.concatenate([even[:, phalf:], odd[:, phalf:]], axis=1),
    )

    def class_of(lens):
        return sum(jnp.where(lens > float(bound), 1.0, 0.0) for bound in BOUNDS)

    lens_down = jnp.transpose(jnp.broadcast_to(lens, (pcount, pcount)))
    class_down = class_of(lens_down)
    p_down = lax.broadcasted_iota(I32, (pcount, LANES), 0).astype(F32)
    lane = lax.broadcasted_iota(I32, (pcount, LANES), 1).astype(F32)
    ahead = jnp.where(class_of(lens) * pcount + lane < class_down * pcount + p_down, 1.0, 0.0).astype(BF16)
    base = jnp.dot(ahead, blocks.astype(BF16), preferred_element_type=F32)
    block_of = jnp.floor(rank * 0.125)
    keyed = jnp.concatenate(
        [jnp.where(hit > 0, block_of, 128.0).astype(BF16), (rank - 8.0 * block_of).astype(BF16)], axis=1
    )
    q_down = lax.broadcasted_iota(I32, (qcount, LANES), 0).astype(F32)
    ends = [
        jnp.sum(jnp.where(class_down <= float(i), blocks, 0.0), axis=0, keepdims=True).astype(I32)
        for i in range(len(BOUNDS) + 1)
    ]

    def list_tile(j):
        slot = lane + float(j * LANES)
        owner = jnp.where(jnp.logical_and(slot >= base, slot < base + blocks), 1.0, 0.0)
        passage = jnp.sum(owner * p_down, axis=0, keepdims=True)
        first = jnp.sum(owner * base, axis=0, keepdims=True)
        length = jnp.sum(owner * lens_down, axis=0, keepdims=True)
        owners[j] = owner.astype(BF16)
        weights = jnp.concatenate([(owner * 8.0).astype(BF16), owner.astype(BF16)], axis=0)
        seen = jnp.dot(keyed, weights, preferred_element_type=F32) - 8.0 * (slot[:1] - first)
        ranks[j] = seen
        rows = [jnp.sum(jnp.where(seen == float(k), q_down, 0.0), axis=0, keepdims=True) for k in range(8)]
        rows = [jnp.clip(r.astype(I32), 0, qcount - 1) for r in rows]
        rows += [jnp.clip(passage.astype(I32), 0, pcount - 1)] + ends + [length.astype(I32)]
        for k, r in enumerate(rows):
            lists[k : k + 1, j * LANES : (j + 1) * LANES] = r

    for h in halves:
        c[h].wait_recv()
        d[h].wait_recv()
        second_axis(h, 3, 2)
    for h in halves:
        push(h, 3, 2, 0, full, None)
    for j in range(tiles // 2):
        list_tile(j)
    for j in (1, 2):
        second_forward(j)
    for j in (1, 2):
        second_near(j)
    for j in range(tiles // 2, tiles):
        list_tile(j)
    second_forward(3)
    second_near(3)
    give_pass.wait_recv()
    relay(1 - core)
    for i, (j, h) in enumerate((j, h) for j in range(4) for h in halves):
        last[2 * i].wait_recv()
        last[2 * i + 1].wait_recv()
        push(h, 6 + 4 * j, shift[j], 2, full, None)
    for wait in waits:
        wait()
    each(lambda copy: copy.wait_send())
    give_pass.wait_send()
    give_len.wait_send()
    fetch_q.wait()


def gather(queries, candidates, passages, lengths, count):
    block, qtok, dim = queries.shape
    plen, pcount, _ = passages.shape
    most = (2 * 3 * candidates.size + 7 * pcount) // 8
    tiles = -(-(most + UNROLL - 1) // LANES)
    vmem, hbm = pl.BlockSpec(memory_space=pltpu.VMEM), pl.BlockSpec(memory_space=pl.ANY)
    dma = pltpu.SemaphoreType.DMA
    args = [pltpu.with_memory_space_constraint(v, pltpu.HBM) for v in (queries, candidates, passages, lengths)]
    return pl.pallas_call(
        functools.partial(gather_kernel, count),
        out_shape=(
            jax.ShapeDtypeStruct((count * block, qtok, dim), BF16),
            jax.ShapeDtypeStruct((pcount, plen, dim), BF16),
            jax.ShapeDtypeStruct((16, tiles * LANES), I32),
            jax.ShapeDtypeStruct((tiles, count * block, LANES), F32),
            jax.ShapeDtypeStruct((tiles, pcount, LANES), BF16),
        ),
        in_specs=[hbm] * 4,
        out_specs=(vmem,) * 5,
        scratch_shapes=[
            pltpu.VMEM(candidates.shape, I32),
            pltpu.VMEM((1, pcount), I32),
            pltpu.VMEM((1, pcount), I32),
            pltpu.VMEM((count, block, pcount), F32),
            pltpu.VMEM((count, block, pcount), BF16),
            pltpu.VMEM((count * block, pcount), BF16),
            pltpu.VMEM((plen, pcount, dim), BF16),
            dma((2, 20)),
            dma((2, 20)),
            dma((2, 20)),
            dma((2, 20)),
            dma((count,)),
            dma((count,)),
            dma((4,)),
            dma((2,)),
            dma((2,)),
        ],
        compiler_params=pltpu.CompilerParams(collective_id=0, has_side_effects=True, vmem_limit_bytes=28 << 20),
        name="gather",
    )(*args)


def score_kernel(qall, pbuf, lists, ranks, owners, out, acc, table, sem):
    qcount, qtok, dim = qall.shape
    pcount, plen, _ = pbuf.shape
    move = pltpu.make_async_copy(lists, table, sem)
    move.start()
    move.wait()
    start = 0
    for c, rows in enumerate(BOUNDS + (plen,)):
        end = table[9 + c, 0]
        down = lax.broadcasted_iota(I32, (rows, 1), 0)

        def step(i, _, start=start, rows=rows, down=down):
            for u in range(UNROLL):
                b = start + i * UNROLL + u
                tokens = jnp.concatenate([qall[table[k, b]] for k in range(8)], axis=0)
                similar = nt(pbuf[table[8, b], :rows], tokens)
                similar = jnp.where(down < table[13, b], similar, -1e30)
                acc[pl.ds(b, 1), :] = jnp.max(similar, axis=0, keepdims=True)
            return 0

        lax.fori_loop(0, (end - start + UNROLL - 1) // UNROLL, step, 0)
        start = end
    token = lax.broadcasted_iota(I32, (8, 8 * qtok), 1)
    mean = jnp.where(token // qtok == lax.broadcasted_iota(I32, (8, 8 * qtok), 0), 1.0 / qtok, 0.0).astype(BF16)
    out[...] = jnp.zeros_like(out)

    def spread(j, _):
        best = acc[pl.ds(pl.multiple_of(j * LANES, LANES), LANES), :]
        high = best.astype(BF16)
        scores = nt(mean, high) + nt(mean, (best - high.astype(F32)).astype(BF16))
        seen = ranks[j]
        dense = sum(jnp.where(seen == float(k), scores[k : k + 1], 0.0) for k in range(8))
        high = dense.astype(BF16)
        both = jnp.concatenate([high, (dense - high.astype(F32)).astype(BF16)], axis=1)
        out[...] += nt(both, jnp.concatenate([owners[j]] * 2, axis=1))
        return 0

    lax.fori_loop(0, (start + LANES - 1) // LANES, spread, 0)


def score(every, passages, lists, ranks, owners):
    qcount, qtok, _ = every.shape
    pcount = passages.shape[0]
    slots = lists.shape[1]
    vmem = pl.BlockSpec(memory_space=pltpu.VMEM)
    return pl.pallas_call(
        score_kernel,
        out_shape=jax.ShapeDtypeStruct((qcount, pcount), F32),
        in_specs=[vmem] * 5,
        out_specs=vmem,
        scratch_shapes=[
            pltpu.VMEM((slots, 8 * qtok), F32),
            pltpu.SMEM((16, slots), I32),
            pltpu.SemaphoreType.DMA,
        ],
        compiler_params=pltpu.CompilerParams(vmem_limit_bytes=20 << 20),
        name="score",
    )(every, passages, lists, ranks, owners)


def return_kernel(count, pcount, dense, cand_ref, out, slabs, send, recv):
    me = lax.axis_index("shard")
    block, ids = cand_ref.shape
    meet(me, count)()

    def slab_copy(k):
        peer = (me + k) % count
        return pltpu.make_async_remote_copy(
            src_ref=dense.at[pl.ds(pl.multiple_of(peer * block, block), block)],
            dst_ref=slabs.at[me],
            send_sem=send.at[k],
            recv_sem=recv.at[k],
            device_id={"shard": peer},
            device_id_type=MESH,
        )

    def each(action):
        def go(k, _):
            action(slab_copy(k))
            return 0

        lax.fori_loop(1, count, go, 0)

    each(lambda copy: copy.start())
    slabs[me] = dense[pl.ds(pl.multiple_of(me * block, block), block), :]
    owner, local = place_of(cand_ref[...], pcount)
    local = jnp.concatenate([local] * (pcount // ids), axis=1)
    each(lambda copy: copy.wait())
    total = jnp.zeros((block, ids), F32)
    for o in range(count):
        found = jnp.take_along_axis(slabs[o], local, axis=1)[:, :ids]
        total = jnp.where(owner == o, found, total)
    out[...] = total


def give_back(dense, candidates, count):
    block, ids = candidates.shape
    pcount = dense.shape[1]
    vmem = pl.BlockSpec(memory_space=pltpu.VMEM)
    dma = pltpu.SemaphoreType.DMA
    return pl.pallas_call(
        functools.partial(return_kernel, count, pcount),
        out_shape=jax.ShapeDtypeStruct((block, ids), F32),
        in_specs=[vmem, vmem],
        out_specs=vmem,
        scratch_shapes=[pltpu.VMEM((count, block, pcount), F32), dma((count,)), dma((count,))],
        compiler_params=pltpu.CompilerParams(collective_id=1, has_side_effects=True, vmem_limit_bytes=8 << 20),
        name="give_back",
    )(dense, candidates)


def shards(queries, passages, lengths, candidates):
    count = lax.axis_size("shard")
    tokens_first = jnp.swapaxes(passages, 0, 1)
    every, kept, lists, ranks, owners = gather(queries, candidates, tokens_first, lengths.reshape(1, -1), count)
    return give_back(score(every, kept, lists, ranks, owners), candidates, count)


def solution(mesh):
    in_specs = (
        P(("group", "shard"), None, None),
        P("shard", None, None),
        P("shard"),
        P(("group", "shard"), None),
    )
    out_specs = P(("group", "shard"), None)
    return jax.shard_map(shards, mesh=mesh, in_specs=in_specs, out_specs=out_specs, check_vma=False)
```

```python
import functools

import jax
import jax.numpy as jnp
from jax import lax
from jax.experimental import pallas as pl
from jax.experimental.pallas import tpu as pltpu
from jax.sharding import PartitionSpec as P

F32, BF16, I32 = jnp.float32, jnp.bfloat16, jnp.int32
MESH = pl.DeviceIdType.MESH
SIDE = 4
LANES = 128
UNROLL = 16
ROOM = 256
BOUNDS = (48, 96, 144)


def nt(a, b):
    return lax.dot_general(a, b, (((1,), (1,)), ((), ())), preferred_element_type=F32)


def place_of(cand, pass_dev):
    half = pass_dev // 2
    within = cand % pass_dev
    owner = cand // (2 * pass_dev) * 2 + within // half
    return owner, cand // pass_dev % 2 * half + within % half


def meet(me, count):
    barrier = pltpu.get_barrier_semaphore()

    def tell(k, _):
        pl.semaphore_signal(barrier, inc=1, device_id={"shard": (me + k) % count}, device_id_type=MESH)
        return 0

    lax.fori_loop(1, count, tell, 0)
    return lambda: pl.semaphore_wait(barrier, count - 1)


def gather_kernel(
    count,
    q_ref,
    cand_ref,
    pass_ref,
    len_ref,
    qall,
    pbuf,
    lists,
    ranks,
    owners,
    pairs_q,
    pairs_p,
    spots,
    cand_buf,
    lens_near,
    lens_far,
    slabs,
    table,
    codes_q,
    codes_p,
    hits,
    stage,
    send,
    recv,
    near_send,
    near_recv,
    slab_send,
    slab_recv,
    own_sem,
    pass_send,
    pass_recv,
):
    me = lax.axis_index("shard")
    core, x, y = me % 2, (me // 2) % SIDE, me // (2 * SIDE)
    block, ids = cand_ref.shape
    plen, pcount, dim = pass_ref.shape
    qcount = qall.shape[0]
    tiles = ranks.shape[0]
    slots = tiles * LANES
    part, phalf = block // 2, pcount // 2
    sibling = me + 1 - 2 * core
    arrive = meet(me, count)
    own_half = pl.ds(pl.multiple_of(core * phalf, phalf), phalf)
    other_half = pl.ds(pl.multiple_of((1 - core) * phalf, phalf), phalf)
    fetch_cand = pltpu.make_async_copy(cand_ref, cand_buf, own_sem.at[0])
    fetch_pass = pltpu.make_async_copy(pass_ref.at[:, own_half, :], stage.at[:, own_half, :], own_sem.at[1])
    fetch_q = pltpu.make_async_copy(q_ref, qall.at[pl.ds(me * block, block)], own_sem.at[2])
    fetch_len = pltpu.make_async_copy(len_ref, lens_near, own_sem.at[3])
    for fetch in (fetch_cand, fetch_pass, fetch_q, fetch_len):
        fetch.start()

    arrive()

    def device(half, first, second):
        px, py = (first, second) if half == 0 else (second, first)
        return ((py + SIDE) % SIDE * SIDE + (px + SIDE) % SIDE) * 2 + core

    pos = ((x, y), (y, x))
    waits = []

    def push(half, index, first, second, piece, target, own=False):
        a, b = pos[half]
        offset = half * part + piece[0]
        start = device(half, a + first, b + second) * block + offset
        dst = qall.at[pl.ds(start, piece[1])]
        near = target is None
        copy = pltpu.make_async_remote_copy(
            src_ref=q_ref.at[pl.ds(offset, piece[1])] if own else dst,
            dst_ref=dst,
            send_sem=(near_send if near else send).at[half, index],
            recv_sem=(near_recv if near else recv).at[half, index],
            device_id={"shard": sibling if near else device(half, a + target[0], b + target[1])},
            device_id_type=MESH,
        )
        copy.start()
        waits.append(copy.wait_send)
        if near:
            waits.append(copy.wait_recv)
        return copy

    def slab_copy(k):
        peer = (me + k) % count
        return pltpu.make_async_remote_copy(
            src_ref=slabs.at[peer],
            dst_ref=table.at[me],
            send_sem=slab_send.at[k],
            recv_sem=slab_recv.at[k],
            device_id={"shard": peer},
            device_id_type=MESH,
        )

    def each(action):
        def go(k, _):
            action(slab_copy(k))
            return 0

        lax.fori_loop(1, count, go, 0)

    full, low, high = (0, part), (0, part // 2), (part // 2, part // 2)
    halves = (0, 1)
    a = [push(h, 0, 0, 0, full, (1, 0), True) for h in halves]
    b = [push(h, 1, 0, 0, full, (-1, 0), True) for h in halves]
    up, down_ = {}, {}

    def second_axis(h, j, offset):
        up[h, j] = push(h, 4 + 4 * j, offset, 0, full, (0, 1), j == 0)
        down_[h, j] = push(h, 5 + 4 * j, offset, 0, full, (0, -1), j == 0)

    for h in halves:
        second_axis(h, 0, 0)
    c = [push(h, 2, 0, 0, full, (2, 0), True) for h in halves]

    def to_sibling(src, dst, index):
        copy = pltpu.make_async_remote_copy(
            src_ref=src,
            dst_ref=dst,
            send_sem=pass_send.at[index],
            recv_sem=pass_recv.at[index],
            device_id={"shard": sibling},
            device_id_type=MESH,
        )
        copy.start()
        return copy

    give_pass = to_sibling(pass_ref.at[:, other_half, :], stage.at[:, own_half, :], 0)
    give_len = to_sibling(len_ref, lens_far, 1)
    for h in halves:
        push(h, 0, 0, 0, full, None, True)

    fetch_cand.wait()
    owner, local = place_of(cand_buf[...], pcount)
    local = local.astype(F32)
    down = lax.broadcasted_iota(I32, (count, ids), 0)
    by_owner = [jnp.where(owner[q : q + 1] == down, 1.0, 0.0) for q in range(block)]
    stack = jnp.concatenate(by_owner, axis=0).astype(BF16)
    earlier = lax.broadcasted_iota(I32, (ids, ids), 0) < lax.broadcasted_iota(I32, (ids, ids), 1)
    prior = jnp.dot(stack, jnp.where(earlier, 1.0, 0.0).astype(BF16), preferred_element_type=F32)
    totals = jnp.dot(stack, jnp.ones((ids, ids), BF16), preferred_element_type=F32)
    running = jnp.zeros((count, ids), F32)
    spot = []
    for q in range(block):
        spot.append(jnp.sum(by_owner[q] * (prior[q * count : (q + 1) * count] + running), axis=0, keepdims=True))
        running = running + totals[q * count : (q + 1) * count]
    spot = jnp.concatenate(spot, axis=0)
    spots[...] = spot.astype(I32)
    spot_down = jnp.transpose(spot).astype(I32)
    across = lax.broadcasted_iota(I32, (ids, ROOM), 1)
    code = jnp.zeros((count, ROOM), F32)
    for q in range(block):
        values = jnp.concatenate([by_owner[q] * local[q : q + 1], by_owner[q]], axis=0).astype(BF16)
        put = jnp.where(spot_down[:, q : q + 1] == across, 1.0, 0.0).astype(BF16)
        found = jnp.dot(values, put, preferred_element_type=F32)
        code = code + found[:count] + found[count:] * float(pcount * (q + 1))
    slabs[:, 0, :] = code
    each(lambda copy: copy.start())
    table[me] = slabs[me]

    def relay(which):
        first = which * phalf

        def go(i, _):
            p = pl.multiple_of(first + i % (phalf // 16) * 16, 16)
            t = pl.multiple_of(i // (phalf // 16) * 16, 16)
            pbuf[pl.ds(p, 16), pl.ds(t, 16), :] = jnp.swapaxes(stage[pl.ds(t, 16), pl.ds(p, 16), :], 0, 1)
            return 0

        lax.fori_loop(0, plen // 16 * (phalf // 16), go, 0)
        rest = plen // 16 * 16
        if rest < plen:
            for i in range(phalf // 16):
                p = pl.multiple_of(first + i * 16, 16)
                pbuf[pl.ds(p, 16), rest:plen, :] = jnp.swapaxes(stage[rest:plen, pl.ds(p, 16), :], 0, 1)

    fetch_pass.wait()
    relay(core)

    shift = (0, -1, 1, 2)
    last = []

    def second_forward(j):
        for h in halves:
            up[h, j].wait_recv()
            last.append(push(h, 6 + 4 * j, shift[j], -1, low, (0, 1)))
            down_[h, j].wait_recv()
            last.append(push(h, 7 + 4 * j, shift[j], 1, high, (0, -1)))

    def second_near(j):
        for h in halves:
            push(h, 4 + 4 * j, shift[j], -1, full, None)
            push(h, 5 + 4 * j, shift[j], 1, full, None)

    for h in halves:
        a[h].wait_recv()
        second_axis(h, 1, -1)
        b[h].wait_recv()
        second_axis(h, 2, 1)
    second_forward(0)
    for h in halves:
        c[h].wait_recv()
        second_axis(h, 3, 2)
    for h in halves:
        push(h, 1, -1, 0, full, None)
        push(h, 2, 1, 0, full, None)
        push(h, 3, 2, 0, full, None)
    second_near(0)

    each(lambda copy: copy.wait_recv())
    codes = table[:, 0, :]
    which_q = jnp.floor(codes * (1.0 / pcount))
    codes_q[...] = which_q - 1.0
    codes_p[...] = codes - which_q * pcount

    def unpack(i, _):
        q_iota = lax.broadcasted_iota(I32, (block, ROOM), 0).astype(F32)
        p_iota = lax.broadcasted_iota(I32, (pcount, ROOM), 0).astype(F32)
        is_q = jnp.where(codes_q[pl.ds(i, 1), :] == q_iota, 1.0, 0.0).astype(BF16)
        is_p = jnp.where(codes_p[pl.ds(i, 1), :] == p_iota, 1.0, 0.0).astype(BF16)
        pairs_q[i] = is_q
        pairs_p[i] = is_p
        hits[pl.ds(pl.multiple_of(i * block, block), block), :] = nt(is_q, is_p).astype(BF16)
        return 0

    lax.fori_loop(0, count, unpack, 0, unroll=8)
    hit = hits[...]
    row = lax.broadcasted_iota(I32, (qcount, qcount), 0)
    col = lax.broadcasted_iota(I32, (qcount, qcount), 1)
    rank = jnp.dot(jnp.where(col < row, 1.0, 0.0).astype(BF16), hit, preferred_element_type=F32)
    number = lax.dot_general(hit, jnp.ones((qcount, pcount), BF16), (((0,), (0,)), ((), ())), preferred_element_type=F32)
    blocks = jnp.floor((number + 7.0) * 0.125)
    fetch_len.wait()
    give_len.wait_recv()
    mine, theirs = lens_near[...].astype(F32), lens_far[...].astype(F32)
    even, odd = jnp.where(core == 0, mine, theirs), jnp.where(core == 0, theirs, mine)
    lens = jnp.where(
        core == 0,
        jnp.concatenate([even[:, :phalf], odd[:, :phalf]], axis=1),
        jnp.concatenate([even[:, phalf:], odd[:, phalf:]], axis=1),
    )

    def class_of(lens):
        return sum(jnp.where(lens > float(bound), 1.0, 0.0) for bound in BOUNDS)

    lens_down = jnp.transpose(jnp.broadcast_to(lens, (pcount, pcount)))
    class_down = class_of(lens_down)
    p_down = lax.broadcasted_iota(I32, (pcount, LANES), 0).astype(F32)
    lane = lax.broadcasted_iota(I32, (pcount, LANES), 1).astype(F32)
    ahead = jnp.where(class_of(lens) * pcount + lane < class_down * pcount + p_down, 1.0, 0.0).astype(BF16)
    base = jnp.dot(ahead, blocks.astype(BF16), preferred_element_type=F32)
    block_of = jnp.floor(rank * 0.125)
    keyed = jnp.concatenate(
        [jnp.where(hit > 0, block_of, 128.0).astype(BF16), (rank - 8.0 * block_of).astype(BF16)], axis=1
    )
    q_down = lax.broadcasted_iota(I32, (qcount, LANES), 0).astype(F32)
    ends = [
        jnp.sum(jnp.where(class_down <= float(i), blocks, 0.0), axis=0, keepdims=True).astype(I32)
        for i in range(len(BOUNDS) + 1)
    ]

    def list_tile(j):
        slot = lane + float(j * LANES)
        owner = jnp.where(jnp.logical_and(slot >= base, slot < base + blocks), 1.0, 0.0)
        passage = jnp.sum(owner * p_down, axis=0, keepdims=True)
        first = jnp.sum(owner * base, axis=0, keepdims=True)
        length = jnp.sum(owner * lens_down, axis=0, keepdims=True)
        owners[j] = owner.astype(BF16)
        weights = jnp.concatenate([(owner * 8.0).astype(BF16), owner.astype(BF16)], axis=0)
        seen = jnp.dot(keyed, weights, preferred_element_type=F32) - 8.0 * (slot[:1] - first)
        ranks[j] = seen
        rows = [jnp.sum(jnp.where(seen == float(k), q_down, 0.0), axis=0, keepdims=True) for k in range(8)]
        rows = [jnp.clip(r.astype(I32), 0, qcount - 1) for r in rows]
        rows += [jnp.clip(passage.astype(I32), 0, pcount - 1)] + ends + [length.astype(I32)]
        for k, r in enumerate(rows):
            lists[k : k + 1, j * LANES : (j + 1) * LANES] = r

    for j in range(tiles // 2):
        list_tile(j)
    for j in (1, 2):
        second_forward(j)
    for j in (1, 2):
        second_near(j)
    for j in range(tiles // 2, tiles):
        list_tile(j)
    second_forward(3)
    second_near(3)
    give_pass.wait_recv()
    relay(1 - core)
    for i, (j, h) in enumerate((j, h) for j in range(4) for h in halves):
        last[2 * i].wait_recv()
        last[2 * i + 1].wait_recv()
        push(h, 6 + 4 * j, shift[j], 2, full, None)
    for wait in waits:
        wait()
    each(lambda copy: copy.wait_send())
    give_pass.wait_send()
    give_len.wait_send()
    fetch_q.wait()


def gather(queries, candidates, passages, lengths, count):
    block, qtok, dim = queries.shape
    plen, pcount, _ = passages.shape
    most = (2 * 3 * candidates.size + 7 * pcount) // 8
    tiles = -(-(most + UNROLL - 1) // LANES)
    vmem, hbm = pl.BlockSpec(memory_space=pltpu.VMEM), pl.BlockSpec(memory_space=pl.ANY)
    dma = pltpu.SemaphoreType.DMA
    args = [pltpu.with_memory_space_constraint(v, pltpu.HBM) for v in (queries, candidates, passages, lengths)]
    return pl.pallas_call(
        functools.partial(gather_kernel, count),
        out_shape=(
            jax.ShapeDtypeStruct((count * block, qtok, dim), BF16),
            jax.ShapeDtypeStruct((pcount, plen, dim), BF16),
            jax.ShapeDtypeStruct((16, tiles * LANES), I32),
            jax.ShapeDtypeStruct((tiles, count * block, LANES), F32),
            jax.ShapeDtypeStruct((tiles, pcount, LANES), BF16),
            jax.ShapeDtypeStruct((count, block, ROOM), BF16),
            jax.ShapeDtypeStruct((count, pcount, ROOM), BF16),
            jax.ShapeDtypeStruct(candidates.shape, I32),
        ),
        in_specs=[hbm] * 4,
        out_specs=(vmem,) * 8,
        scratch_shapes=[
            pltpu.VMEM(candidates.shape, I32),
            pltpu.VMEM((1, pcount), I32),
            pltpu.VMEM((1, pcount), I32),
            pltpu.VMEM((count, 1, ROOM), F32),
            pltpu.VMEM((count, 1, ROOM), F32),
            pltpu.VMEM((count, ROOM), F32),
            pltpu.VMEM((count, ROOM), F32),
            pltpu.VMEM((count * block, pcount), BF16),
            pltpu.VMEM((plen, pcount, dim), BF16),
            dma((2, 20)),
            dma((2, 20)),
            dma((2, 20)),
            dma((2, 20)),
            dma((count,)),
            dma((count,)),
            dma((4,)),
            dma((2,)),
            dma((2,)),
        ],
        compiler_params=pltpu.CompilerParams(collective_id=0, has_side_effects=True, vmem_limit_bytes=28 << 20),
        name="gather",
    )(*args)


def score_kernel(qall, pbuf, lists, ranks, owners, pairs_q, pairs_p, out, acc, total, table, sem):
    qcount, qtok, dim = qall.shape
    pcount, plen, _ = pbuf.shape
    move = pltpu.make_async_copy(lists, table, sem)
    move.start()
    move.wait()
    start = 0
    for c, rows in enumerate(BOUNDS + (plen,)):
        end = table[9 + c, 0]
        down = lax.broadcasted_iota(I32, (rows, 1), 0)

        def step(i, _, start=start, rows=rows, down=down):
            for u in range(UNROLL):
                b = start + i * UNROLL + u
                tokens = jnp.concatenate([qall[table[k, b]] for k in range(8)], axis=0)
                similar = nt(pbuf[table[8, b], :rows], tokens)
                similar = jnp.where(down < table[13, b], similar, -1e30)
                acc[pl.ds(b, 1), :] = jnp.max(similar, axis=0, keepdims=True)
            return 0

        whole = (end - start + (UNROLL - 1 if rows == plen else 0)) // UNROLL
        lax.fori_loop(0, whole, step, 0)
        start = start + whole * UNROLL
    token = lax.broadcasted_iota(I32, (8, 8 * qtok), 1)
    mean = jnp.where(token // qtok == lax.broadcasted_iota(I32, (8, 8 * qtok), 0), 1.0 / qtok, 0.0).astype(BF16)
    total[...] = jnp.zeros_like(total)

    def spread(j, _):
        best = acc[pl.ds(pl.multiple_of(j * LANES, LANES), LANES), :]
        high = best.astype(BF16)
        scores = nt(mean, high) + nt(mean, (best - high.astype(F32)).astype(BF16))
        seen = ranks[j]
        dense = sum(jnp.where(seen == float(k), scores[k : k + 1], 0.0) for k in range(8))
        high = dense.astype(BF16)
        both = jnp.concatenate([high, (dense - high.astype(F32)).astype(BF16)], axis=1)
        total[...] += nt(both, jnp.concatenate([owners[j]] * 2, axis=1))
        return 0

    lax.fori_loop(0, (table[9 + len(BOUNDS), 0] + LANES - 1) // LANES, spread, 0)
    count, block, _ = pairs_q.shape

    def pack(i, _):
        rows = total[pl.ds(pl.multiple_of(i * block, block), block), :]
        high = rows.astype(BF16)
        both = jnp.concatenate([high, (rows - high.astype(F32)).astype(BF16)], axis=0)
        found = jnp.dot(both, pairs_p[i], preferred_element_type=F32)
        found = (found[:block] + found[block:]) * pairs_q[i].astype(F32)
        out[i] = jnp.sum(found, axis=0, keepdims=True)
        return 0

    lax.fori_loop(0, count, pack, 0, unroll=8)


def score(every, passages, lists, ranks, owners, pairs_q, pairs_p):
    qcount, qtok, _ = every.shape
    pcount = passages.shape[0]
    slots = lists.shape[1]
    vmem = pl.BlockSpec(memory_space=pltpu.VMEM)
    return pl.pallas_call(
        score_kernel,
        out_shape=jax.ShapeDtypeStruct((pairs_q.shape[0], 1, ROOM), F32),
        in_specs=[vmem] * 7,
        out_specs=vmem,
        scratch_shapes=[
            pltpu.VMEM((slots, 8 * qtok), F32),
            pltpu.VMEM((qcount, pcount), F32),
            pltpu.SMEM((16, slots), I32),
            pltpu.SemaphoreType.DMA,
        ],
        compiler_params=pltpu.CompilerParams(vmem_limit_bytes=20 << 20),
        name="score",
    )(every, passages, lists, ranks, owners, pairs_q, pairs_p)


def return_kernel(count, pcount, compact, cand_ref, spots, out, slabs, send, recv):
    me = lax.axis_index("shard")
    block, ids = cand_ref.shape
    arrive = meet(me, count)
    owner, _ = place_of(cand_ref[...], pcount)
    spot = spots[...]
    spot_w = jnp.concatenate([spot % LANES] * (LANES // ids), axis=1)
    arrive()

    def slab_copy(k):
        peer = (me + k) % count
        return pltpu.make_async_remote_copy(
            src_ref=compact.at[peer],
            dst_ref=slabs.at[me],
            send_sem=send.at[k],
            recv_sem=recv.at[k],
            device_id={"shard": peer},
            device_id_type=MESH,
        )

    def each(action):
        def go(k, _):
            action(slab_copy(k))
            return 0

        lax.fori_loop(1, count, go, 0)

    each(lambda copy: copy.start())
    slabs[me] = compact[me]
    each(lambda copy: copy.wait())
    result = jnp.zeros((block, ids), F32)
    for o in range(count):
        for part in range(ROOM // LANES):
            row = jnp.broadcast_to(slabs[o, :, part * LANES : (part + 1) * LANES], (block, LANES))
            found = jnp.take_along_axis(row, spot_w, axis=1)[:, :ids]
            result = jnp.where(jnp.logical_and(owner == o, spot // LANES == part), found, result)
    out[...] = result


def give_back(compact, candidates, spots, pcount):
    block, ids = candidates.shape
    count = compact.shape[0]
    vmem = pl.BlockSpec(memory_space=pltpu.VMEM)
    dma = pltpu.SemaphoreType.DMA
    return pl.pallas_call(
        functools.partial(return_kernel, count, pcount),
        out_shape=jax.ShapeDtypeStruct((block, ids), F32),
        in_specs=[vmem] * 3,
        out_specs=vmem,
        scratch_shapes=[pltpu.VMEM((count, 1, ROOM), F32), dma((count,)), dma((count,))],
        compiler_params=pltpu.CompilerParams(collective_id=1, has_side_effects=True, vmem_limit_bytes=8 << 20),
        name="give_back",
    )(compact, candidates, spots)


def shards(queries, passages, lengths, candidates):
    count = lax.axis_size("shard")
    tokens_first = jnp.swapaxes(passages, 0, 1)
    *made, spots = gather(queries, candidates, tokens_first, lengths.reshape(1, -1), count)
    return give_back(score(*made), candidates, spots, passages.shape[0])


def solution(mesh):
    in_specs = (
        P(("group", "shard"), None, None),
        P("shard", None, None),
        P("shard"),
        P(("group", "shard"), None),
    )
    out_specs = P(("group", "shard"), None)
    return jax.shard_map(shards, mesh=mesh, in_specs=in_specs, out_specs=out_specs, check_vma=False)
```

```python
import functools

import jax
import jax.numpy as jnp
from jax import lax
from jax.experimental import pallas as pl
from jax.experimental.pallas import tpu as pltpu
from jax.sharding import PartitionSpec as P

F32, BF16, I32 = jnp.float32, jnp.bfloat16, jnp.int32
MESH = pl.DeviceIdType.MESH
SIDE = 4
LANES = 128
UNROLL = 16
EARLY = 3
ROOM = 256
BOUNDS = (48, 96, 144)


def nt(a, b):
    return lax.dot_general(a, b, (((1,), (1,)), ((), ())), preferred_element_type=F32)


def place_of(cand, pass_dev):
    half = pass_dev // 2
    within = cand % pass_dev
    owner = cand // (2 * pass_dev) * 2 + within // half
    return owner, cand // pass_dev % 2 * half + within % half


def meet(me, count):
    barrier = pltpu.get_barrier_semaphore()

    def tell(k, _):
        pl.semaphore_signal(barrier, inc=1, device_id={"shard": (me + k) % count}, device_id_type=MESH)
        return 0

    lax.fori_loop(1, count, tell, 0)
    return lambda: pl.semaphore_wait(barrier, count - 1)


def gather_kernel(
    count,
    q_ref,
    cand_ref,
    pass_ref,
    len_ref,
    qall,
    pbuf,
    lists,
    ranks,
    owners,
    pairs_q,
    pairs_p,
    spots,
    cand_buf,
    lens_near,
    lens_far,
    slabs,
    table,
    codes_q,
    codes_p,
    hits,
    stage,
    send,
    recv,
    near_send,
    near_recv,
    slab_send,
    slab_recv,
    own_sem,
    pass_send,
    pass_recv,
):
    me = lax.axis_index("shard")
    core, x, y = me % 2, (me // 2) % SIDE, me // (2 * SIDE)
    block, ids = cand_ref.shape
    plen, pcount, dim = pass_ref.shape
    qcount = qall.shape[0]
    tiles = ranks.shape[0]
    slots = tiles * LANES
    part, phalf = block // 2, pcount // 2
    sibling = me + 1 - 2 * core
    arrive = meet(me, count)
    own_half = pl.ds(pl.multiple_of(core * phalf, phalf), phalf)
    other_half = pl.ds(pl.multiple_of((1 - core) * phalf, phalf), phalf)
    fetch_cand = pltpu.make_async_copy(cand_ref, cand_buf, own_sem.at[0])
    fetch_pass = pltpu.make_async_copy(pass_ref.at[:, own_half, :], stage.at[:, own_half, :], own_sem.at[1])
    fetch_q = pltpu.make_async_copy(q_ref, qall.at[pl.ds(me * block, block)], own_sem.at[2])
    fetch_len = pltpu.make_async_copy(len_ref, lens_near, own_sem.at[3])
    for fetch in (fetch_cand, fetch_pass, fetch_q, fetch_len):
        fetch.start()

    arrive()

    def device(half, first, second):
        px, py = (first, second) if half == 0 else (second, first)
        return ((py + SIDE) % SIDE * SIDE + (px + SIDE) % SIDE) * 2 + core

    pos = ((x, y), (y, x))
    waits = []

    def push(half, index, first, second, piece, target, own=False):
        a, b = pos[half]
        offset = half * part + piece[0]
        start = device(half, a + first, b + second) * block + offset
        dst = qall.at[pl.ds(start, piece[1])]
        near = target is None
        copy = pltpu.make_async_remote_copy(
            src_ref=q_ref.at[pl.ds(offset, piece[1])] if own else dst,
            dst_ref=dst,
            send_sem=(near_send if near else send).at[half, index],
            recv_sem=(near_recv if near else recv).at[half, index],
            device_id={"shard": sibling if near else device(half, a + target[0], b + target[1])},
            device_id_type=MESH,
        )
        copy.start()
        waits.append(copy.wait_send)
        if near:
            waits.append(copy.wait_recv)
        return copy

    def slab_copy(k):
        peer = (me + k) % count
        return pltpu.make_async_remote_copy(
            src_ref=slabs.at[peer],
            dst_ref=table.at[me],
            send_sem=slab_send.at[k],
            recv_sem=slab_recv.at[k],
            device_id={"shard": peer},
            device_id_type=MESH,
        )

    def each(action):
        def go(k, _):
            action(slab_copy(k))
            return 0

        lax.fori_loop(1, count, go, 0)

    full, low, high = (0, part), (0, part // 2), (part // 2, part // 2)
    halves = (0, 1)
    a = [push(h, 0, 0, 0, full, (1, 0), True) for h in halves]
    b = [push(h, 1, 0, 0, full, (-1, 0), True) for h in halves]
    up, down_ = {}, {}

    def second_axis(h, j, offset):
        up[h, j] = push(h, 4 + 4 * j, offset, 0, full, (0, 1), j == 0)
        down_[h, j] = push(h, 5 + 4 * j, offset, 0, full, (0, -1), j == 0)

    for h in halves:
        second_axis(h, 0, 0)
    c = [push(h, 2, 0, 0, full, (2, 0), True) for h in halves]

    def to_sibling(src, dst, index):
        copy = pltpu.make_async_remote_copy(
            src_ref=src,
            dst_ref=dst,
            send_sem=pass_send.at[index],
            recv_sem=pass_recv.at[index],
            device_id={"shard": sibling},
            device_id_type=MESH,
        )
        copy.start()
        return copy

    give_pass = to_sibling(pass_ref.at[:, other_half, :], stage.at[:, own_half, :], 0)
    give_len = to_sibling(len_ref, lens_far, 1)
    for h in halves:
        push(h, 0, 0, 0, full, None, True)

    fetch_cand.wait()
    owner, local = place_of(cand_buf[...], pcount)
    local = local.astype(F32)
    down = lax.broadcasted_iota(I32, (count, ids), 0)
    by_owner = [jnp.where(owner[q : q + 1] == down, 1.0, 0.0) for q in range(block)]
    stack = jnp.concatenate(by_owner, axis=0).astype(BF16)
    earlier = lax.broadcasted_iota(I32, (ids, ids), 0) < lax.broadcasted_iota(I32, (ids, ids), 1)
    prior = jnp.dot(stack, jnp.where(earlier, 1.0, 0.0).astype(BF16), preferred_element_type=F32)
    totals = jnp.dot(stack, jnp.ones((ids, ids), BF16), preferred_element_type=F32)
    running = jnp.zeros((count, ids), F32)
    spot = []
    for q in range(block):
        spot.append(jnp.sum(by_owner[q] * (prior[q * count : (q + 1) * count] + running), axis=0, keepdims=True))
        running = running + totals[q * count : (q + 1) * count]
    spot = jnp.concatenate(spot, axis=0)
    spots[...] = spot.astype(I32)
    spot_down = jnp.transpose(spot).astype(I32)
    across = lax.broadcasted_iota(I32, (ids, ROOM), 1)
    code = jnp.zeros((count, ROOM), F32)
    for q in range(block):
        values = jnp.concatenate([by_owner[q] * local[q : q + 1], by_owner[q]], axis=0).astype(BF16)
        put = jnp.where(spot_down[:, q : q + 1] == across, 1.0, 0.0).astype(BF16)
        found = jnp.dot(values, put, preferred_element_type=F32)
        code = code + found[:count] + found[count:] * float(pcount * (q + 1))
    slabs[:, 0, :] = code
    each(lambda copy: copy.start())
    table[me] = slabs[me]

    def relay(which):
        first = which * phalf

        def go(i, _):
            p = pl.multiple_of(first + i % (phalf // 16) * 16, 16)
            t = pl.multiple_of(i // (phalf // 16) * 16, 16)
            pbuf[pl.ds(p, 16), pl.ds(t, 16), :] = jnp.swapaxes(stage[pl.ds(t, 16), pl.ds(p, 16), :], 0, 1)
            return 0

        lax.fori_loop(0, plen // 16 * (phalf // 16), go, 0)
        rest = plen // 16 * 16
        if rest < plen:
            for i in range(phalf // 16):
                p = pl.multiple_of(first + i * 16, 16)
                pbuf[pl.ds(p, 16), rest:plen, :] = jnp.swapaxes(stage[rest:plen, pl.ds(p, 16), :], 0, 1)

    fetch_pass.wait()
    relay(core)

    shift = (0, -1, 1, 2)
    last = []

    def second_forward(j):
        for h in halves:
            up[h, j].wait_recv()
            last.append(push(h, 6 + 4 * j, shift[j], -1, low, (0, 1)))
            down_[h, j].wait_recv()
            last.append(push(h, 7 + 4 * j, shift[j], 1, high, (0, -1)))

    def second_near(j):
        for h in halves:
            push(h, 4 + 4 * j, shift[j], -1, full, None)
            push(h, 5 + 4 * j, shift[j], 1, full, None)

    for h in halves:
        a[h].wait_recv()
        second_axis(h, 1, -1)
        b[h].wait_recv()
        second_axis(h, 2, 1)
    second_forward(0)
    for h in halves:
        c[h].wait_recv()
        second_axis(h, 3, 2)
    for h in halves:
        push(h, 1, -1, 0, full, None)
        push(h, 2, 1, 0, full, None)
        push(h, 3, 2, 0, full, None)
    second_near(0)

    each(lambda copy: copy.wait_recv())
    codes = table[:, 0, :]
    which_q = jnp.floor(codes * (1.0 / pcount))
    codes_q[...] = which_q - 1.0
    codes_p[...] = codes - which_q * pcount

    def unpack(i, _):
        q_iota = lax.broadcasted_iota(I32, (block, ROOM), 0).astype(F32)
        p_iota = lax.broadcasted_iota(I32, (pcount, ROOM), 0).astype(F32)
        is_q = jnp.where(codes_q[pl.ds(i, 1), :] == q_iota, 1.0, 0.0).astype(BF16)
        is_p = jnp.where(codes_p[pl.ds(i, 1), :] == p_iota, 1.0, 0.0).astype(BF16)
        pairs_q[i] = is_q
        pairs_p[i] = is_p
        hits[pl.ds(pl.multiple_of(i * block, block), block), :] = nt(is_q, is_p).astype(BF16)
        return 0

    lax.fori_loop(0, count, unpack, 0, unroll=8)
    hit = hits[...]
    row = lax.broadcasted_iota(I32, (qcount, qcount), 0)
    col = lax.broadcasted_iota(I32, (qcount, qcount), 1)
    rank = jnp.dot(jnp.where(col < row, 1.0, 0.0).astype(BF16), hit, preferred_element_type=F32)
    number = lax.dot_general(hit, jnp.ones((qcount, pcount), BF16), (((0,), (0,)), ((), ())), preferred_element_type=F32)
    blocks = jnp.floor((number + 7.0) * 0.125)
    fetch_len.wait()
    give_len.wait_recv()
    mine, theirs = lens_near[...].astype(F32), lens_far[...].astype(F32)
    even, odd = jnp.where(core == 0, mine, theirs), jnp.where(core == 0, theirs, mine)
    lens = jnp.where(
        core == 0,
        jnp.concatenate([even[:, :phalf], odd[:, :phalf]], axis=1),
        jnp.concatenate([even[:, phalf:], odd[:, phalf:]], axis=1),
    )

    def class_of(lens):
        return sum(jnp.where(lens > float(bound), 1.0, 0.0) for bound in BOUNDS)

    lens_down = jnp.transpose(jnp.broadcast_to(lens, (pcount, pcount)))
    class_down = class_of(lens_down)
    p_down = lax.broadcasted_iota(I32, (pcount, LANES), 0).astype(F32)
    lane = lax.broadcasted_iota(I32, (pcount, LANES), 1).astype(F32)
    ahead = jnp.where(class_of(lens) * pcount + lane < class_down * pcount + p_down, 1.0, 0.0).astype(BF16)
    base = jnp.dot(ahead, blocks.astype(BF16), preferred_element_type=F32)
    block_of = jnp.floor(rank * 0.125)
    keyed = jnp.concatenate(
        [jnp.where(hit > 0, block_of, 128.0).astype(BF16), (rank - 8.0 * block_of).astype(BF16)], axis=1
    )
    q_down = lax.broadcasted_iota(I32, (qcount, LANES), 0).astype(F32)
    ends = [
        jnp.sum(jnp.where(class_down <= float(i), blocks, 0.0), axis=0, keepdims=True).astype(I32)
        for i in range(len(BOUNDS) + 1)
    ]

    def list_tile(j):
        slot = lane + float(j * LANES)
        owner = jnp.where(jnp.logical_and(slot >= base, slot < base + blocks), 1.0, 0.0)
        passage = jnp.sum(owner * p_down, axis=0, keepdims=True)
        first = jnp.sum(owner * base, axis=0, keepdims=True)
        length = jnp.sum(owner * lens_down, axis=0, keepdims=True)
        owners[j] = owner.astype(BF16)
        weights = jnp.concatenate([(owner * 8.0).astype(BF16), owner.astype(BF16)], axis=0)
        used = jnp.sum(owner, axis=0, keepdims=True)
        seen = jnp.dot(keyed, weights, preferred_element_type=F32) - 8.0 * (slot[:1] - first)
        seen = seen - 16.0 * qcount * (1.0 - used)
        ranks[j] = seen
        rows = [jnp.sum(jnp.where(seen == float(k), q_down, 0.0), axis=0, keepdims=True) for k in range(8)]
        rows = [jnp.clip(r.astype(I32), 0, qcount - 1) for r in rows]
        rows += [jnp.clip(passage.astype(I32), 0, pcount - 1)] + ends + [length.astype(I32)]
        for k, r in enumerate(rows):
            lists[k : k + 1, j * LANES : (j + 1) * LANES] = r

    for j in (1, 2):
        second_forward(j)
    for j in (1, 2):
        second_near(j)
    for j in range(0, 4):
        list_tile(j)
    second_forward(3)
    second_near(3)
    for j in range(4, tiles):
        list_tile(j)
    give_pass.wait_recv()
    relay(1 - core)
    for i, (j, h) in enumerate((j, h) for j in range(4) for h in halves):
        last[2 * i].wait_recv()
        last[2 * i + 1].wait_recv()
        push(h, 6 + 4 * j, shift[j], 2, full, None)
    for wait in waits:
        wait()
    each(lambda copy: copy.wait_send())
    give_pass.wait_send()
    give_len.wait_send()
    fetch_q.wait()


def gather(queries, candidates, passages, lengths, count):
    block, qtok, dim = queries.shape
    plen, pcount, _ = passages.shape
    most = (2 * 3 * candidates.size + 7 * pcount) // 8
    tiles = -(-(most + UNROLL - 1) // LANES)
    vmem, hbm = pl.BlockSpec(memory_space=pltpu.VMEM), pl.BlockSpec(memory_space=pl.ANY)
    dma = pltpu.SemaphoreType.DMA
    args = [pltpu.with_memory_space_constraint(v, pltpu.HBM) for v in (queries, candidates, passages, lengths)]
    return pl.pallas_call(
        functools.partial(gather_kernel, count),
        out_shape=(
            jax.ShapeDtypeStruct((count * block, qtok, dim), BF16),
            jax.ShapeDtypeStruct((pcount, plen, dim), BF16),
            jax.ShapeDtypeStruct((16, tiles * LANES), I32),
            jax.ShapeDtypeStruct((tiles, count * block, LANES), F32),
            jax.ShapeDtypeStruct((tiles, pcount, LANES), BF16),
            jax.ShapeDtypeStruct((count, block, ROOM), BF16),
            jax.ShapeDtypeStruct((count, pcount, ROOM), BF16),
            jax.ShapeDtypeStruct(candidates.shape, I32),
        ),
        in_specs=[hbm] * 4,
        out_specs=(vmem,) * 8,
        scratch_shapes=[
            pltpu.VMEM(candidates.shape, I32),
            pltpu.VMEM((1, pcount), I32),
            pltpu.VMEM((1, pcount), I32),
            pltpu.VMEM((count, 1, ROOM), F32),
            pltpu.VMEM((count, 1, ROOM), F32),
            pltpu.VMEM((count, ROOM), F32),
            pltpu.VMEM((count, ROOM), F32),
            pltpu.VMEM((count * block, pcount), BF16),
            pltpu.VMEM((plen, pcount, dim), BF16),
            dma((2, 20)),
            dma((2, 20)),
            dma((2, 20)),
            dma((2, 20)),
            dma((count,)),
            dma((count,)),
            dma((4,)),
            dma((2,)),
            dma((2,)),
        ],
        compiler_params=pltpu.CompilerParams(collective_id=0, has_side_effects=True, vmem_limit_bytes=28 << 20),
        name="gather",
    )(*args)


def score_kernel(qall, pbuf, lists, ranks, owners, acc, total, table, sem):
    qcount, qtok, dim = qall.shape
    pcount, plen, _ = pbuf.shape
    move = pltpu.make_async_copy(lists, table, sem)
    move.start()
    move.wait()
    start = 0
    for c, rows in enumerate(BOUNDS + (plen,)):
        end = table[9 + c, 0]
        down = lax.broadcasted_iota(I32, (rows, 1), 0)

        def step(i, _, start=start, rows=rows, down=down):
            for u in range(UNROLL):
                b = start + i * UNROLL + u
                tokens = jnp.concatenate([qall[table[k, b]] for k in range(8)], axis=0)
                similar = nt(pbuf[table[8, b], :rows], tokens)
                similar = jnp.where(down < table[13, b], similar, -1e30)
                acc[pl.ds(b, 1), :] = jnp.max(similar, axis=0, keepdims=True)
            return 0

        whole = (end - start + (UNROLL - 1 if rows == plen else 0)) // UNROLL
        lax.fori_loop(0, whole, step, 0)
        start = start + whole * UNROLL
    total[...] = jnp.zeros_like(total)

    def late(j, _):
        spread(j, acc, ranks, owners, total, qtok)
        return 0

    lax.fori_loop(EARLY, (table[9 + len(BOUNDS), 0] + LANES - 1) // LANES, late, 0)


def spread(j, acc, ranks, owners, total, qtok):
    token = lax.broadcasted_iota(I32, (8, 8 * qtok), 1)
    mean = jnp.where(token // qtok == lax.broadcasted_iota(I32, (8, 8 * qtok), 0), 1.0 / qtok, 0.0).astype(BF16)
    best = acc[pl.ds(pl.multiple_of(j * LANES, LANES), LANES), :]
    high = best.astype(BF16)
    scores = nt(mean, high) + nt(mean, (best - high.astype(F32)).astype(BF16))
    seen = ranks[j]
    dense = sum(jnp.where(seen == float(k), scores[k : k + 1], 0.0) for k in range(8))
    high = dense.astype(BF16)
    both = jnp.concatenate([high, (dense - high.astype(F32)).astype(BF16)], axis=1)
    total[...] += nt(both, jnp.concatenate([owners[j]] * 2, axis=1))


def score(every, passages, lists, ranks, owners):
    qcount, qtok, _ = every.shape
    pcount = passages.shape[0]
    slots = lists.shape[1]
    vmem = pl.BlockSpec(memory_space=pltpu.VMEM)
    return pl.pallas_call(
        score_kernel,
        out_shape=(
            jax.ShapeDtypeStruct((slots, 8 * qtok), F32),
            jax.ShapeDtypeStruct((qcount, pcount), F32),
        ),
        in_specs=[vmem] * 5,
        out_specs=(vmem, vmem),
        scratch_shapes=[
            pltpu.SMEM((16, slots), I32),
            pltpu.SemaphoreType.DMA,
        ],
        compiler_params=pltpu.CompilerParams(vmem_limit_bytes=20 << 20),
        name="score",
    )(every, passages, lists, ranks, owners)


def return_kernel(
    count, acc, partial, ranks, owners, pairs_q, pairs_p, cand_ref, spots, out, total, compact, slabs, send, recv
):
    me = lax.axis_index("shard")
    block, ids = cand_ref.shape
    arrive = meet(me, count)
    total[...] = partial[...]
    for j in range(EARLY):
        spread(j, acc, ranks, owners, total, acc.shape[1] // 8)

    def pack(i, _):
        rows = total[pl.ds(pl.multiple_of(i * block, block), block), :]
        high = rows.astype(BF16)
        both = jnp.concatenate([high, (rows - high.astype(F32)).astype(BF16)], axis=0)
        found = jnp.dot(both, pairs_p[i], preferred_element_type=F32)
        found = (found[:block] + found[block:]) * pairs_q[i].astype(F32)
        compact[i] = jnp.sum(found, axis=0, keepdims=True)
        return 0

    lax.fori_loop(0, count, pack, 0, unroll=8)
    owner, _ = place_of(cand_ref[...], partial.shape[1])
    spot = spots[...]
    spot_w = jnp.concatenate([spot % LANES] * (LANES // ids), axis=1)
    arrive()

    def slab_copy(k):
        peer = (me + k) % count
        return pltpu.make_async_remote_copy(
            src_ref=compact.at[peer],
            dst_ref=slabs.at[me],
            send_sem=send.at[k],
            recv_sem=recv.at[k],
            device_id={"shard": peer},
            device_id_type=MESH,
        )

    def each(action):
        def go(k, _):
            action(slab_copy(k))
            return 0

        lax.fori_loop(1, count, go, 0)

    each(lambda copy: copy.start())
    slabs[me] = compact[me]
    each(lambda copy: copy.wait())
    result = jnp.zeros((block, ids), F32)
    for o in range(count):
        for part in range(ROOM // LANES):
            row = jnp.broadcast_to(slabs[o, :, part * LANES : (part + 1) * LANES], (block, LANES))
            found = jnp.take_along_axis(row, spot_w, axis=1)[:, :ids]
            result = jnp.where(jnp.logical_and(owner == o, spot // LANES == part), found, result)
    out[...] = result


def give_back(acc, partial, ranks, owners, pairs_q, pairs_p, candidates, spots):
    block, ids = candidates.shape
    count = pairs_q.shape[0]
    vmem = pl.BlockSpec(memory_space=pltpu.VMEM)
    dma = pltpu.SemaphoreType.DMA
    return pl.pallas_call(
        functools.partial(return_kernel, count),
        out_shape=jax.ShapeDtypeStruct((block, ids), F32),
        in_specs=[vmem] * 8,
        out_specs=vmem,
        scratch_shapes=[
            pltpu.VMEM(partial.shape, F32),
            pltpu.VMEM((count, 1, ROOM), F32),
            pltpu.VMEM((count, 1, ROOM), F32),
            dma((count,)),
            dma((count,)),
        ],
        compiler_params=pltpu.CompilerParams(collective_id=1, has_side_effects=True, vmem_limit_bytes=8 << 20),
        name="give_back",
    )(acc, partial, ranks, owners, pairs_q, pairs_p, candidates, spots)


def shards(queries, passages, lengths, candidates):
    count = lax.axis_size("shard")
    tokens_first = jnp.swapaxes(passages, 0, 1)
    every, kept, lists, ranks, owners, pairs_q, pairs_p, spots = gather(
        queries, candidates, tokens_first, lengths.reshape(1, -1), count
    )
    best, partial = score(every, kept, lists, ranks, owners)
    return give_back(best, partial, ranks, owners, pairs_q, pairs_p, candidates, spots)


def solution(mesh):
    in_specs = (
        P(("group", "shard"), None, None),
        P("shard", None, None),
        P("shard"),
        P(("group", "shard"), None),
    )
    out_specs = P(("group", "shard"), None)
    return jax.shard_map(shards, mesh=mesh, in_specs=in_specs, out_specs=out_specs, check_vma=False)
```

```python
import functools

import jax
import jax.numpy as jnp
from jax import lax
from jax.experimental import pallas as pl
from jax.experimental.pallas import tpu as pltpu
from jax.sharding import PartitionSpec as P

F32, BF16, I32 = jnp.float32, jnp.bfloat16, jnp.int32
MESH = pl.DeviceIdType.MESH
SIDE = 4
LANES = 128
UNROLL = 16
EARLY = 3
ROOM = 256
BOUNDS = (48, 96, 144)


def nt(a, b):
    return lax.dot_general(a, b, (((1,), (1,)), ((), ())), preferred_element_type=F32)


def place_of(cand, pass_dev):
    half = pass_dev // 2
    within = cand % pass_dev
    owner = cand // (2 * pass_dev) * 2 + within // half
    return owner, cand // pass_dev % 2 * half + within % half


def meet(me, count):
    barrier = pltpu.get_barrier_semaphore()

    def tell(k, _):
        pl.semaphore_signal(barrier, inc=1, device_id={"shard": (me + k) % count}, device_id_type=MESH)
        return 0

    lax.fori_loop(1, count, tell, 0, unroll=True)
    return lambda: pl.semaphore_wait(barrier, count - 1)


def gather_kernel(
    count,
    q_ref,
    cand_ref,
    pass_ref,
    len_ref,
    qall,
    pbuf,
    lists,
    ranks,
    owners,
    pairs_q,
    pairs_p,
    spots,
    cand_buf,
    lens_near,
    lens_far,
    slabs,
    table,
    codes_q,
    codes_p,
    hits,
    stage,
    send,
    recv,
    near_send,
    near_recv,
    slab_send,
    slab_recv,
    own_sem,
    pass_send,
    pass_recv,
):
    me = lax.axis_index("shard")
    core, x, y = me % 2, (me // 2) % SIDE, me // (2 * SIDE)
    block, ids = cand_ref.shape
    plen, pcount, dim = pass_ref.shape
    qcount = qall.shape[0]
    tiles = ranks.shape[0]
    slots = tiles * LANES
    part, phalf = block // 2, pcount // 2
    sibling = me + 1 - 2 * core
    arrive = meet(me, count)
    own_half = pl.ds(pl.multiple_of(core * phalf, phalf), phalf)
    other_half = pl.ds(pl.multiple_of((1 - core) * phalf, phalf), phalf)
    fetch_cand = pltpu.make_async_copy(cand_ref, cand_buf, own_sem.at[0])
    fetch_pass = pltpu.make_async_copy(pass_ref.at[:, own_half, :], stage.at[:, own_half, :], own_sem.at[1])
    fetch_q = pltpu.make_async_copy(q_ref, qall.at[pl.ds(me * block, block)], own_sem.at[2])
    fetch_len = pltpu.make_async_copy(len_ref, lens_near, own_sem.at[3])
    for fetch in (fetch_cand, fetch_pass, fetch_q, fetch_len):
        fetch.start()

    arrive()

    def device(half, first, second):
        px, py = (first, second) if half == 0 else (second, first)
        return ((py + SIDE) % SIDE * SIDE + (px + SIDE) % SIDE) * 2 + core

    pos = ((x, y), (y, x))
    waits = []

    def push(half, index, first, second, piece, target, own=False):
        a, b = pos[half]
        offset = half * part + piece[0]
        start = device(half, a + first, b + second) * block + offset
        dst = qall.at[pl.ds(start, piece[1])]
        near = target is None
        copy = pltpu.make_async_remote_copy(
            src_ref=q_ref.at[pl.ds(offset, piece[1])] if own else dst,
            dst_ref=dst,
            send_sem=(near_send if near else send).at[half, index],
            recv_sem=(near_recv if near else recv).at[half, index],
            device_id={"shard": sibling if near else device(half, a + target[0], b + target[1])},
            device_id_type=MESH,
        )
        copy.start()
        waits.append(copy.wait_send)
        if near:
            waits.append(copy.wait_recv)
        return copy

    def slab_copy(k):
        peer = (me + k) % count
        return pltpu.make_async_remote_copy(
            src_ref=slabs.at[peer],
            dst_ref=table.at[me],
            send_sem=slab_send.at[k],
            recv_sem=slab_recv.at[k],
            device_id={"shard": peer},
            device_id_type=MESH,
        )

    def each(action):
        def go(k, _):
            action(slab_copy(k))
            return 0

        lax.fori_loop(1, count, go, 0, unroll=True)

    full, low, high = (0, part), (0, part // 2), (part // 2, part // 2)
    halves = (0, 1)
    a = [push(h, 0, 0, 0, full, (1, 0), True) for h in halves]
    b = [push(h, 1, 0, 0, full, (-1, 0), True) for h in halves]
    up, down_ = {}, {}

    def second_axis(h, j, offset):
        up[h, j] = push(h, 4 + 4 * j, offset, 0, full, (0, 1), j == 0)
        down_[h, j] = push(h, 5 + 4 * j, offset, 0, full, (0, -1), j == 0)

    for h in halves:
        second_axis(h, 0, 0)
    c = [push(h, 2, 0, 0, full, (2, 0), True) for h in halves]

    def to_sibling(src, dst, index):
        copy = pltpu.make_async_remote_copy(
            src_ref=src,
            dst_ref=dst,
            send_sem=pass_send.at[index],
            recv_sem=pass_recv.at[index],
            device_id={"shard": sibling},
            device_id_type=MESH,
        )
        copy.start()
        return copy

    give_pass = to_sibling(pass_ref.at[:, other_half, :], stage.at[:, own_half, :], 0)
    give_len = to_sibling(len_ref, lens_far, 1)
    for h in halves:
        push(h, 0, 0, 0, full, None, True)

    fetch_cand.wait()
    owner, local = place_of(cand_buf[...], pcount)
    local = local.astype(F32)
    down = lax.broadcasted_iota(I32, (count, ids), 0)
    by_owner = [jnp.where(owner[q : q + 1] == down, 1.0, 0.0) for q in range(block)]
    stack = jnp.concatenate(by_owner, axis=0).astype(BF16)
    earlier = lax.broadcasted_iota(I32, (ids, ids), 0) < lax.broadcasted_iota(I32, (ids, ids), 1)
    prior = jnp.dot(stack, jnp.where(earlier, 1.0, 0.0).astype(BF16), preferred_element_type=F32)
    totals = jnp.dot(stack, jnp.ones((ids, ids), BF16), preferred_element_type=F32)
    running = jnp.zeros((count, ids), F32)
    spot = []
    for q in range(block):
        spot.append(jnp.sum(by_owner[q] * (prior[q * count : (q + 1) * count] + running), axis=0, keepdims=True))
        running = running + totals[q * count : (q + 1) * count]
    spot = jnp.concatenate(spot, axis=0)
    spots[...] = spot.astype(I32)
    spot_down = jnp.transpose(spot).astype(I32)
    across = lax.broadcasted_iota(I32, (ids, ROOM), 1)
    code = jnp.zeros((count, ROOM), F32)
    for q in range(block):
        values = jnp.concatenate([by_owner[q] * local[q : q + 1], by_owner[q]], axis=0).astype(BF16)
        put = jnp.where(spot_down[:, q : q + 1] == across, 1.0, 0.0).astype(BF16)
        found = jnp.dot(values, put, preferred_element_type=F32)
        code = code + found[:count] + found[count:] * float(pcount * (q + 1))
    slabs[:, 0, :] = code
    each(lambda copy: copy.start())
    table[me] = slabs[me]

    def relay(which):
        first = which * phalf

        def go(i, _):
            p = pl.multiple_of(first + i % (phalf // 16) * 16, 16)
            t = pl.multiple_of(i // (phalf // 16) * 16, 16)
            pbuf[pl.ds(p, 16), pl.ds(t, 16), :] = jnp.swapaxes(stage[pl.ds(t, 16), pl.ds(p, 16), :], 0, 1)
            return 0

        lax.fori_loop(0, plen // 16 * (phalf // 16), go, 0, unroll=4)
        rest = plen // 16 * 16
        if rest < plen:
            for i in range(phalf // 16):
                p = pl.multiple_of(first + i * 16, 16)
                pbuf[pl.ds(p, 16), rest:plen, :] = jnp.swapaxes(stage[rest:plen, pl.ds(p, 16), :], 0, 1)

    fetch_pass.wait()
    relay(core)

    shift = (0, -1, 1, 2)
    last = []

    def second_forward(j):
        for h in halves:
            up[h, j].wait_recv()
            last.append(push(h, 6 + 4 * j, shift[j], -1, low, (0, 1)))
            down_[h, j].wait_recv()
            last.append(push(h, 7 + 4 * j, shift[j], 1, high, (0, -1)))

    def second_near(j):
        for h in halves:
            push(h, 4 + 4 * j, shift[j], -1, full, None)
            push(h, 5 + 4 * j, shift[j], 1, full, None)

    for h in halves:
        a[h].wait_recv()
        second_axis(h, 1, -1)
        b[h].wait_recv()
        second_axis(h, 2, 1)
    second_forward(0)
    for h in halves:
        c[h].wait_recv()
        second_axis(h, 3, 2)
    for h in halves:
        push(h, 1, -1, 0, full, None)
        push(h, 2, 1, 0, full, None)
        push(h, 3, 2, 0, full, None)
    second_near(0)

    each(lambda copy: copy.wait_recv())
    codes = table[:, 0, :]
    which_q = jnp.floor(codes * (1.0 / pcount))
    codes_q[...] = which_q - 1.0
    codes_p[...] = codes - which_q * pcount

    def unpack(i, _):
        q_iota = lax.broadcasted_iota(I32, (block, ROOM), 0).astype(F32)
        p_iota = lax.broadcasted_iota(I32, (pcount, ROOM), 0).astype(F32)
        is_q = jnp.where(codes_q[pl.ds(i, 1), :] == q_iota, 1.0, 0.0).astype(BF16)
        is_p = jnp.where(codes_p[pl.ds(i, 1), :] == p_iota, 1.0, 0.0).astype(BF16)
        pairs_q[i] = is_q
        pairs_p[i] = is_p
        hits[pl.ds(pl.multiple_of(i * block, block), block), :] = nt(is_q, is_p).astype(BF16)
        return 0

    lax.fori_loop(0, count, unpack, 0, unroll=8)
    hit = hits[...]
    row = lax.broadcasted_iota(I32, (qcount, qcount), 0)
    col = lax.broadcasted_iota(I32, (qcount, qcount), 1)
    rank = jnp.dot(jnp.where(col < row, 1.0, 0.0).astype(BF16), hit, preferred_element_type=F32)
    number = lax.dot_general(hit, jnp.ones((qcount, pcount), BF16), (((0,), (0,)), ((), ())), preferred_element_type=F32)
    blocks = jnp.floor((number + 7.0) * 0.125)
    fetch_len.wait()
    give_len.wait_recv()
    mine, theirs = lens_near[...].astype(F32), lens_far[...].astype(F32)
    even, odd = jnp.where(core == 0, mine, theirs), jnp.where(core == 0, theirs, mine)
    lens = jnp.where(
        core == 0,
        jnp.concatenate([even[:, :phalf], odd[:, :phalf]], axis=1),
        jnp.concatenate([even[:, phalf:], odd[:, phalf:]], axis=1),
    )

    def class_of(lens):
        return sum(jnp.where(lens > float(bound), 1.0, 0.0) for bound in BOUNDS)

    lens_down = jnp.transpose(jnp.broadcast_to(lens, (pcount, pcount)))
    class_down = class_of(lens_down)
    p_down = lax.broadcasted_iota(I32, (pcount, LANES), 0).astype(F32)
    lane = lax.broadcasted_iota(I32, (pcount, LANES), 1).astype(F32)
    ahead = jnp.where(class_of(lens) * pcount + lane < class_down * pcount + p_down, 1.0, 0.0).astype(BF16)
    base = jnp.dot(ahead, blocks.astype(BF16), preferred_element_type=F32)
    block_of = jnp.floor(rank * 0.125)
    keyed = jnp.concatenate(
        [jnp.where(hit > 0, block_of, 128.0).astype(BF16), (rank - 8.0 * block_of).astype(BF16)], axis=1
    )
    q_down = lax.broadcasted_iota(I32, (qcount, LANES), 0).astype(F32)
    ends = [
        jnp.sum(jnp.where(class_down <= float(i), blocks, 0.0), axis=0, keepdims=True).astype(I32)
        for i in range(len(BOUNDS) + 1)
    ]

    def list_tile(j):
        slot = lane + float(j * LANES)
        owner = jnp.where(jnp.logical_and(slot >= base, slot < base + blocks), 1.0, 0.0)
        passage = jnp.sum(owner * p_down, axis=0, keepdims=True)
        first = jnp.sum(owner * base, axis=0, keepdims=True)
        length = jnp.sum(owner * lens_down, axis=0, keepdims=True)
        owners[j] = owner.astype(BF16)
        weights = jnp.concatenate([(owner * 8.0).astype(BF16), owner.astype(BF16)], axis=0)
        used = jnp.sum(owner, axis=0, keepdims=True)
        seen = jnp.dot(keyed, weights, preferred_element_type=F32) - 8.0 * (slot[:1] - first)
        seen = seen - 16.0 * qcount * (1.0 - used)
        ranks[j] = seen
        rows = [jnp.sum(jnp.where(seen == float(k), q_down, 0.0), axis=0, keepdims=True) for k in range(8)]
        rows = [jnp.clip(r.astype(I32), 0, qcount - 1) for r in rows]
        rows += [jnp.clip(passage.astype(I32), 0, pcount - 1)] + ends + [length.astype(I32)]
        for k, r in enumerate(rows):
            lists[k : k + 1, j * LANES : (j + 1) * LANES] = r

    for j in (1, 2):
        second_forward(j)
    for j in (1, 2):
        second_near(j)
    for j in range(0, 4):
        list_tile(j)
    second_forward(3)
    second_near(3)
    for j in range(4, tiles):
        list_tile(j)
    give_pass.wait_recv()
    relay(1 - core)
    for i, (j, h) in enumerate((j, h) for j in range(4) for h in halves):
        last[2 * i].wait_recv()
        last[2 * i + 1].wait_recv()
        push(h, 6 + 4 * j, shift[j], 2, full, None)
    for wait in waits:
        wait()
    each(lambda copy: copy.wait_send())
    give_pass.wait_send()
    give_len.wait_send()
    fetch_q.wait()


def gather(queries, candidates, passages, lengths, count):
    block, qtok, dim = queries.shape
    plen, pcount, _ = passages.shape
    most = (2 * 3 * candidates.size + 7 * pcount) // 8
    tiles = -(-(most + UNROLL - 1) // LANES)
    vmem, hbm = pl.BlockSpec(memory_space=pltpu.VMEM), pl.BlockSpec(memory_space=pl.ANY)
    dma = pltpu.SemaphoreType.DMA
    args = [pltpu.with_memory_space_constraint(v, pltpu.HBM) for v in (queries, candidates, passages, lengths)]
    return pl.pallas_call(
        functools.partial(gather_kernel, count),
        out_shape=(
            jax.ShapeDtypeStruct((count * block, qtok, dim), BF16),
            jax.ShapeDtypeStruct((pcount, plen, dim), BF16),
            jax.ShapeDtypeStruct((16, tiles * LANES), I32),
            jax.ShapeDtypeStruct((tiles, count * block, LANES), F32),
            jax.ShapeDtypeStruct((tiles, pcount, LANES), BF16),
            jax.ShapeDtypeStruct((count, block, ROOM), BF16),
            jax.ShapeDtypeStruct((count, pcount, ROOM), BF16),
            jax.ShapeDtypeStruct(candidates.shape, I32),
        ),
        in_specs=[hbm] * 4,
        out_specs=(vmem,) * 8,
        scratch_shapes=[
            pltpu.VMEM(candidates.shape, I32),
            pltpu.VMEM((1, pcount), I32),
            pltpu.VMEM((1, pcount), I32),
            pltpu.VMEM((count, 1, ROOM), F32),
            pltpu.VMEM((count, 1, ROOM), F32),
            pltpu.VMEM((count, ROOM), F32),
            pltpu.VMEM((count, ROOM), F32),
            pltpu.VMEM((count * block, pcount), BF16),
            pltpu.VMEM((plen, pcount, dim), BF16),
            dma((2, 20)),
            dma((2, 20)),
            dma((2, 20)),
            dma((2, 20)),
            dma((count,)),
            dma((count,)),
            dma((4,)),
            dma((2,)),
            dma((2,)),
        ],
        compiler_params=pltpu.CompilerParams(collective_id=0, has_side_effects=True, vmem_limit_bytes=28 << 20),
        name="gather",
    )(*args)


def score_kernel(qall, pbuf, lists, ranks, owners, acc, total, table, sem):
    qcount, qtok, dim = qall.shape
    pcount, plen, _ = pbuf.shape
    first = EARLY * LANES + UNROLL
    first = (first + LANES - 1) // LANES * LANES
    move = pltpu.make_async_copy(lists.at[:, :first], table.at[:, :first], sem)
    move.start()
    move.wait()

    @pl.when(table[9 + len(BOUNDS), 0] + UNROLL > first)
    def _():
        rest = pltpu.make_async_copy(lists.at[:, first:], table.at[:, first:], sem)
        rest.start()
        rest.wait()

    start = 0
    for c, rows in enumerate(BOUNDS + (plen,)):
        end = table[9 + c, 0]
        down = lax.broadcasted_iota(I32, (rows, 1), 0)

        def step(i, _, start=start, rows=rows, down=down):
            for u in range(UNROLL):
                b = start + i * UNROLL + u
                tokens = jnp.concatenate([qall[table[k, b]] for k in range(8)], axis=0)
                similar = nt(pbuf[table[8, b], :rows], tokens)
                similar = jnp.where(down < table[13, b], similar, -1e30)
                acc[pl.ds(b, 1), :] = jnp.max(similar, axis=0, keepdims=True)
            return 0

        whole = (end - start + (UNROLL - 1 if rows == plen else 0)) // UNROLL
        lax.fori_loop(0, whole, step, 0)
        start = start + whole * UNROLL
    total[...] = jnp.zeros_like(total)

    def late(j, _):
        spread(j, acc, ranks, owners, total, qtok)
        return 0

    lax.fori_loop(EARLY, (table[9 + len(BOUNDS), 0] + LANES - 1) // LANES, late, 0)


def spread(j, acc, ranks, owners, total, qtok):
    token = lax.broadcasted_iota(I32, (8, 8 * qtok), 1)
    mean = jnp.where(token // qtok == lax.broadcasted_iota(I32, (8, 8 * qtok), 0), 1.0 / qtok, 0.0).astype(BF16)
    best = acc[pl.ds(pl.multiple_of(j * LANES, LANES), LANES), :]
    high = best.astype(BF16)
    scores = nt(mean, high) + nt(mean, (best - high.astype(F32)).astype(BF16))
    seen = ranks[j]
    dense = sum(jnp.where(seen == float(k), scores[k : k + 1], 0.0) for k in range(8))
    high = dense.astype(BF16)
    both = jnp.concatenate([high, (dense - high.astype(F32)).astype(BF16)], axis=1)
    total[...] += nt(both, jnp.concatenate([owners[j]] * 2, axis=1))


def score(every, passages, lists, ranks, owners):
    qcount, qtok, _ = every.shape
    pcount = passages.shape[0]
    slots = lists.shape[1]
    vmem = pl.BlockSpec(memory_space=pltpu.VMEM)
    return pl.pallas_call(
        score_kernel,
        out_shape=(
            jax.ShapeDtypeStruct((slots, 8 * qtok), F32),
            jax.ShapeDtypeStruct((qcount, pcount), F32),
        ),
        in_specs=[vmem] * 5,
        out_specs=(vmem, vmem),
        scratch_shapes=[
            pltpu.SMEM((16, slots), I32),
            pltpu.SemaphoreType.DMA,
        ],
        compiler_params=pltpu.CompilerParams(vmem_limit_bytes=20 << 20),
        name="score",
    )(every, passages, lists, ranks, owners)


def return_kernel(
    count, acc, partial, ranks, owners, pairs_q, pairs_p, cand_ref, spots, out, total, compact, slabs, send, recv
):
    me = lax.axis_index("shard")
    block, ids = cand_ref.shape
    arrive = meet(me, count)
    total[...] = partial[...]
    for j in range(EARLY):
        spread(j, acc, ranks, owners, total, acc.shape[1] // 8)

    def pack(i, _):
        rows = total[pl.ds(pl.multiple_of(i * block, block), block), :]
        high = rows.astype(BF16)
        both = jnp.concatenate([high, (rows - high.astype(F32)).astype(BF16)], axis=0)
        found = jnp.dot(both, pairs_p[i], preferred_element_type=F32)
        found = (found[:block] + found[block:]) * pairs_q[i].astype(F32)
        compact[i] = jnp.sum(found, axis=0, keepdims=True)
        return 0

    lax.fori_loop(0, count, pack, 0, unroll=8)
    owner, _ = place_of(cand_ref[...], partial.shape[1])
    spot = spots[...]
    spot_w = jnp.concatenate([spot % LANES] * (LANES // ids), axis=1)
    arrive()

    def slab_copy(k):
        peer = (me + k) % count
        return pltpu.make_async_remote_copy(
            src_ref=compact.at[peer],
            dst_ref=slabs.at[me],
            send_sem=send.at[k],
            recv_sem=recv.at[k],
            device_id={"shard": peer},
            device_id_type=MESH,
        )

    def each(action):
        def go(k, _):
            action(slab_copy(k))
            return 0

        lax.fori_loop(1, count, go, 0, unroll=True)

    each(lambda copy: copy.start())
    slabs[me] = compact[me]
    each(lambda copy: copy.wait())
    result = jnp.zeros((block, ids), F32)
    for o in range(count):
        for part in range(ROOM // LANES):
            row = jnp.broadcast_to(slabs[o, :, part * LANES : (part + 1) * LANES], (block, LANES))
            found = jnp.take_along_axis(row, spot_w, axis=1)[:, :ids]
            result = jnp.where(jnp.logical_and(owner == o, spot // LANES == part), found, result)
    out[...] = result


def give_back(acc, partial, ranks, owners, pairs_q, pairs_p, candidates, spots):
    block, ids = candidates.shape
    count = pairs_q.shape[0]
    vmem = pl.BlockSpec(memory_space=pltpu.VMEM)
    dma = pltpu.SemaphoreType.DMA
    return pl.pallas_call(
        functools.partial(return_kernel, count),
        out_shape=jax.ShapeDtypeStruct((block, ids), F32),
        in_specs=[vmem] * 8,
        out_specs=vmem,
        scratch_shapes=[
            pltpu.VMEM(partial.shape, F32),
            pltpu.VMEM((count, 1, ROOM), F32),
            pltpu.VMEM((count, 1, ROOM), F32),
            dma((count,)),
            dma((count,)),
        ],
        compiler_params=pltpu.CompilerParams(collective_id=1, has_side_effects=True, vmem_limit_bytes=8 << 20),
        name="give_back",
    )(acc, partial, ranks, owners, pairs_q, pairs_p, candidates, spots)


def shards(queries, passages, lengths, candidates):
    count = lax.axis_size("shard")
    tokens_first = jnp.swapaxes(passages, 0, 1)
    every, kept, lists, ranks, owners, pairs_q, pairs_p, spots = gather(
        queries, candidates, tokens_first, lengths.reshape(1, -1), count
    )
    best, partial = score(every, kept, lists, ranks, owners)
    return give_back(best, partial, ranks, owners, pairs_q, pairs_p, candidates, spots)


def solution(mesh):
    in_specs = (
        P(("group", "shard"), None, None),
        P("shard", None, None),
        P("shard"),
        P(("group", "shard"), None),
    )
    out_specs = P(("group", "shard"), None)
    return jax.shard_map(shards, mesh=mesh, in_specs=in_specs, out_specs=out_specs, check_vma=False)
```

```python
import functools

import jax
import jax.numpy as jnp
from jax import lax
from jax.experimental import pallas as pl
from jax.experimental.pallas import tpu as pltpu
from jax.sharding import PartitionSpec as P

F32, BF16, I32 = jnp.float32, jnp.bfloat16, jnp.int32
MESH = pl.DeviceIdType.MESH
SIDE = 4
LANES = 128
UNROLL = 32
EARLY = 3
ROOM = 256
BOUNDS = (48, 96, 144)


def nt(a, b):
    return lax.dot_general(a, b, (((1,), (1,)), ((), ())), preferred_element_type=F32)


def place_of(cand, pass_dev):
    half = pass_dev // 2
    within = cand % pass_dev
    owner = cand // (2 * pass_dev) * 2 + within // half
    return owner, cand // pass_dev % 2 * half + within % half


def meet(me, count):
    barrier = pltpu.get_barrier_semaphore()

    def tell(k, _):
        pl.semaphore_signal(barrier, inc=1, device_id={"shard": (me + k) % count}, device_id_type=MESH)
        return 0

    lax.fori_loop(1, count, tell, 0, unroll=True)
    return lambda: pl.semaphore_wait(barrier, count - 1)


def gather_kernel(
    count,
    q_ref,
    cand_ref,
    pass_ref,
    len_ref,
    qall,
    pbuf,
    lists,
    ranks,
    owners,
    pairs_q,
    pairs_p,
    spots,
    cand_buf,
    lens_near,
    lens_far,
    slabs,
    table,
    codes_q,
    codes_p,
    hits,
    stage,
    send,
    recv,
    near_send,
    near_recv,
    slab_send,
    slab_recv,
    own_sem,
    pass_send,
    pass_recv,
):
    me = lax.axis_index("shard")
    core, x, y = me % 2, (me // 2) % SIDE, me // (2 * SIDE)
    block, ids = cand_ref.shape
    plen, pcount, dim = pass_ref.shape
    qcount = qall.shape[0]
    tiles = ranks.shape[0]
    slots = tiles * LANES
    part, phalf = block // 2, pcount // 2
    sibling = me + 1 - 2 * core
    arrive = meet(me, count)
    own_half = pl.ds(pl.multiple_of(core * phalf, phalf), phalf)
    other_half = pl.ds(pl.multiple_of((1 - core) * phalf, phalf), phalf)
    fetch_cand = pltpu.make_async_copy(cand_ref, cand_buf, own_sem.at[0])
    fetch_pass = pltpu.make_async_copy(pass_ref.at[:, own_half, :], stage.at[:, own_half, :], own_sem.at[1])
    fetch_q = pltpu.make_async_copy(q_ref, qall.at[pl.ds(me * block, block)], own_sem.at[2])
    fetch_len = pltpu.make_async_copy(len_ref, lens_near, own_sem.at[3])
    for fetch in (fetch_cand, fetch_pass, fetch_q, fetch_len):
        fetch.start()

    arrive()

    def device(half, first, second):
        px, py = (first, second) if half == 0 else (second, first)
        return ((py + SIDE) % SIDE * SIDE + (px + SIDE) % SIDE) * 2 + core

    pos = ((x, y), (y, x))
    waits = []

    def push(half, index, first, second, piece, target, own=False):
        a, b = pos[half]
        offset = half * part + piece[0]
        start = device(half, a + first, b + second) * block + offset
        dst = qall.at[pl.ds(start, piece[1])]
        near = target is None
        copy = pltpu.make_async_remote_copy(
            src_ref=q_ref.at[pl.ds(offset, piece[1])] if own else dst,
            dst_ref=dst,
            send_sem=(near_send if near else send).at[half, index],
            recv_sem=(near_recv if near else recv).at[half, index],
            device_id={"shard": sibling if near else device(half, a + target[0], b + target[1])},
            device_id_type=MESH,
        )
        copy.start()
        waits.append(copy.wait_send)
        if near:
            waits.append(copy.wait_recv)
        return copy

    def slab_copy(k):
        peer = (me + k) % count
        return pltpu.make_async_remote_copy(
            src_ref=slabs.at[peer],
            dst_ref=table.at[me],
            send_sem=slab_send.at[k],
            recv_sem=slab_recv.at[k],
            device_id={"shard": peer},
            device_id_type=MESH,
        )

    def each(action):
        def go(k, _):
            action(slab_copy(k))
            return 0

        lax.fori_loop(1, count, go, 0, unroll=True)

    full, low, high = (0, part), (0, part // 2), (part // 2, part // 2)
    halves = (0, 1)
    a = [push(h, 0, 0, 0, full, (1, 0), True) for h in halves]
    b = [push(h, 1, 0, 0, full, (-1, 0), True) for h in halves]
    up, down_ = {}, {}

    def second_axis(h, j, offset):
        up[h, j] = push(h, 4 + 4 * j, offset, 0, full, (0, 1), j == 0)
        down_[h, j] = push(h, 5 + 4 * j, offset, 0, full, (0, -1), j == 0)

    for h in halves:
        second_axis(h, 0, 0)
    c = [push(h, 2, 0, 0, full, (2, 0), True) for h in halves]

    def to_sibling(src, dst, index):
        copy = pltpu.make_async_remote_copy(
            src_ref=src,
            dst_ref=dst,
            send_sem=pass_send.at[index],
            recv_sem=pass_recv.at[index],
            device_id={"shard": sibling},
            device_id_type=MESH,
        )
        copy.start()
        return copy

    give_pass = to_sibling(pass_ref.at[:, other_half, :], stage.at[:, own_half, :], 0)
    give_len = to_sibling(len_ref, lens_far, 1)
    for h in halves:
        push(h, 0, 0, 0, full, None, True)

    fetch_cand.wait()
    owner, local = place_of(cand_buf[...], pcount)
    local = local.astype(F32)
    down = lax.broadcasted_iota(I32, (count, ids), 0)
    by_owner = [jnp.where(owner[q : q + 1] == down, 1.0, 0.0) for q in range(block)]
    stack = jnp.concatenate(by_owner, axis=0).astype(BF16)
    earlier = lax.broadcasted_iota(I32, (ids, ids), 0) < lax.broadcasted_iota(I32, (ids, ids), 1)
    prior = jnp.dot(stack, jnp.where(earlier, 1.0, 0.0).astype(BF16), preferred_element_type=F32)
    totals = jnp.dot(stack, jnp.ones((ids, ids), BF16), preferred_element_type=F32)
    running = jnp.zeros((count, ids), F32)
    spot = []
    for q in range(block):
        spot.append(jnp.sum(by_owner[q] * (prior[q * count : (q + 1) * count] + running), axis=0, keepdims=True))
        running = running + totals[q * count : (q + 1) * count]
    spot = jnp.concatenate(spot, axis=0)
    spots[...] = spot.astype(I32)
    spot_down = jnp.transpose(spot).astype(I32)
    across = lax.broadcasted_iota(I32, (ids, ROOM), 1)
    code = jnp.zeros((count, ROOM), F32)
    for q in range(block):
        values = jnp.concatenate([by_owner[q] * local[q : q + 1], by_owner[q]], axis=0).astype(BF16)
        put = jnp.where(spot_down[:, q : q + 1] == across, 1.0, 0.0).astype(BF16)
        found = jnp.dot(values, put, preferred_element_type=F32)
        code = code + found[:count] + found[count:] * float(pcount * (q + 1))
    slabs[:, 0, :] = code
    each(lambda copy: copy.start())
    table[me] = slabs[me]

    def relay(which):
        first = which * phalf

        def go(i, _):
            p = pl.multiple_of(first + i % (phalf // 16) * 16, 16)
            t = pl.multiple_of(i // (phalf // 16) * 16, 16)
            pbuf[pl.ds(p, 16), pl.ds(t, 16), :] = jnp.swapaxes(stage[pl.ds(t, 16), pl.ds(p, 16), :], 0, 1)
            return 0

        lax.fori_loop(0, plen // 16 * (phalf // 16), go, 0, unroll=4)
        rest = plen // 16 * 16
        if rest < plen:
            for i in range(phalf // 16):
                p = pl.multiple_of(first + i * 16, 16)
                pbuf[pl.ds(p, 16), rest:plen, :] = jnp.swapaxes(stage[rest:plen, pl.ds(p, 16), :], 0, 1)

    fetch_pass.wait()
    relay(core)

    shift = (0, -1, 1, 2)
    last = []

    def second_forward(j):
        for h in halves:
            up[h, j].wait_recv()
            last.append(push(h, 6 + 4 * j, shift[j], -1, low, (0, 1)))
            down_[h, j].wait_recv()
            last.append(push(h, 7 + 4 * j, shift[j], 1, high, (0, -1)))

    def second_near(j):
        for h in halves:
            push(h, 4 + 4 * j, shift[j], -1, full, None)
            push(h, 5 + 4 * j, shift[j], 1, full, None)

    for h in halves:
        a[h].wait_recv()
        second_axis(h, 1, -1)
        b[h].wait_recv()
        second_axis(h, 2, 1)
    second_forward(0)
    for h in halves:
        c[h].wait_recv()
        second_axis(h, 3, 2)
    for h in halves:
        push(h, 1, -1, 0, full, None)
        push(h, 2, 1, 0, full, None)
        push(h, 3, 2, 0, full, None)
    second_near(0)

    each(lambda copy: copy.wait_recv())
    codes = table[:, 0, :]
    which_q = jnp.floor(codes * (1.0 / pcount))
    codes_q[...] = which_q - 1.0
    codes_p[...] = codes - which_q * pcount

    def unpack(i, _):
        q_iota = lax.broadcasted_iota(I32, (block, ROOM), 0).astype(F32)
        p_iota = lax.broadcasted_iota(I32, (pcount, ROOM), 0).astype(F32)
        is_q = jnp.where(codes_q[pl.ds(i, 1), :] == q_iota, 1.0, 0.0).astype(BF16)
        is_p = jnp.where(codes_p[pl.ds(i, 1), :] == p_iota, 1.0, 0.0).astype(BF16)
        pairs_q[i] = is_q
        pairs_p[i] = is_p
        hits[pl.ds(pl.multiple_of(i * block, block), block), :] = nt(is_q, is_p).astype(BF16)
        return 0

    lax.fori_loop(0, count, unpack, 0, unroll=8)
    hit = hits[...]
    row = lax.broadcasted_iota(I32, (qcount, qcount), 0)
    col = lax.broadcasted_iota(I32, (qcount, qcount), 1)
    rank = jnp.dot(jnp.where(col < row, 1.0, 0.0).astype(BF16), hit, preferred_element_type=F32)
    number = lax.dot_general(hit, jnp.ones((qcount, pcount), BF16), (((0,), (0,)), ((), ())), preferred_element_type=F32)
    blocks = jnp.floor((number + 7.0) * 0.125)
    fetch_len.wait()
    give_len.wait_recv()
    mine, theirs = lens_near[...].astype(F32), lens_far[...].astype(F32)
    even, odd = jnp.where(core == 0, mine, theirs), jnp.where(core == 0, theirs, mine)
    lens = jnp.where(
        core == 0,
        jnp.concatenate([even[:, :phalf], odd[:, :phalf]], axis=1),
        jnp.concatenate([even[:, phalf:], odd[:, phalf:]], axis=1),
    )

    def class_of(lens):
        return sum(jnp.where(lens > float(bound), 1.0, 0.0) for bound in BOUNDS)

    lens_down = jnp.transpose(jnp.broadcast_to(lens, (pcount, pcount)))
    class_down = class_of(lens_down)
    p_down = lax.broadcasted_iota(I32, (pcount, LANES), 0).astype(F32)
    lane = lax.broadcasted_iota(I32, (pcount, LANES), 1).astype(F32)
    ahead = jnp.where(class_of(lens) * pcount + lane < class_down * pcount + p_down, 1.0, 0.0).astype(BF16)
    base = jnp.dot(ahead, blocks.astype(BF16), preferred_element_type=F32)
    block_of = jnp.floor(rank * 0.125)
    keyed = jnp.concatenate(
        [jnp.where(hit > 0, block_of, 128.0).astype(BF16), (rank - 8.0 * block_of).astype(BF16)], axis=1
    )
    q_down = lax.broadcasted_iota(I32, (qcount, LANES), 0).astype(F32)
    ends = [
        jnp.sum(jnp.where(class_down <= float(i), blocks, 0.0), axis=0, keepdims=True).astype(I32)
        for i in range(len(BOUNDS) + 1)
    ]

    def list_tile(j):
        slot = lane + float(j * LANES)
        owner = jnp.where(jnp.logical_and(slot >= base, slot < base + blocks), 1.0, 0.0)
        passage = jnp.sum(owner * p_down, axis=0, keepdims=True)
        first = jnp.sum(owner * base, axis=0, keepdims=True)
        length = jnp.sum(owner * lens_down, axis=0, keepdims=True)
        owners[j] = owner.astype(BF16)
        weights = jnp.concatenate([(owner * 8.0).astype(BF16), owner.astype(BF16)], axis=0)
        used = jnp.sum(owner, axis=0, keepdims=True)
        seen = jnp.dot(keyed, weights, preferred_element_type=F32) - 8.0 * (slot[:1] - first)
        seen = seen - 16.0 * qcount * (1.0 - used)
        ranks[j] = seen
        rows = [jnp.sum(jnp.where(seen == float(k), q_down, 0.0), axis=0, keepdims=True) for k in range(8)]
        rows = [jnp.clip(r.astype(I32), 0, qcount - 1) for r in rows]
        rows += [jnp.clip(passage.astype(I32), 0, pcount - 1)] + ends + [length.astype(I32)]
        for k, r in enumerate(rows):
            lists[k : k + 1, j * LANES : (j + 1) * LANES] = r

    for j in (1, 2):
        second_forward(j)
    for j in (1, 2):
        second_near(j)
    for j in range(0, 4):
        list_tile(j)
    second_forward(3)
    second_near(3)
    for j in range(4, tiles):
        list_tile(j)
    give_pass.wait_recv()
    relay(1 - core)
    for i, (j, h) in enumerate((j, h) for j in range(4) for h in halves):
        last[2 * i].wait_recv()
        last[2 * i + 1].wait_recv()
        push(h, 6 + 4 * j, shift[j], 2, full, None)
    for wait in waits:
        wait()
    each(lambda copy: copy.wait_send())
    give_pass.wait_send()
    give_len.wait_send()
    fetch_q.wait()


def gather(queries, candidates, passages, lengths, count):
    block, qtok, dim = queries.shape
    plen, pcount, _ = passages.shape
    most = (2 * 3 * candidates.size + 7 * pcount) // 8
    tiles = -(-(most + UNROLL - 1) // LANES)
    vmem, hbm = pl.BlockSpec(memory_space=pltpu.VMEM), pl.BlockSpec(memory_space=pl.ANY)
    dma = pltpu.SemaphoreType.DMA
    args = [pltpu.with_memory_space_constraint(v, pltpu.HBM) for v in (queries, candidates, passages, lengths)]
    return pl.pallas_call(
        functools.partial(gather_kernel, count),
        out_shape=(
            jax.ShapeDtypeStruct((count * block, qtok, dim), BF16),
            jax.ShapeDtypeStruct((pcount, plen, dim), BF16),
            jax.ShapeDtypeStruct((16, tiles * LANES), I32),
            jax.ShapeDtypeStruct((tiles, count * block, LANES), F32),
            jax.ShapeDtypeStruct((tiles, pcount, LANES), BF16),
            jax.ShapeDtypeStruct((count, block, ROOM), BF16),
            jax.ShapeDtypeStruct((count, pcount, ROOM), BF16),
            jax.ShapeDtypeStruct(candidates.shape, I32),
        ),
        in_specs=[hbm] * 4,
        out_specs=(vmem,) * 8,
        scratch_shapes=[
            pltpu.VMEM(candidates.shape, I32),
            pltpu.VMEM((1, pcount), I32),
            pltpu.VMEM((1, pcount), I32),
            pltpu.VMEM((count, 1, ROOM), F32),
            pltpu.VMEM((count, 1, ROOM), F32),
            pltpu.VMEM((count, ROOM), F32),
            pltpu.VMEM((count, ROOM), F32),
            pltpu.VMEM((count * block, pcount), BF16),
            pltpu.VMEM((plen, pcount, dim), BF16),
            dma((2, 20)),
            dma((2, 20)),
            dma((2, 20)),
            dma((2, 20)),
            dma((count,)),
            dma((count,)),
            dma((4,)),
            dma((2,)),
            dma((2,)),
        ],
        compiler_params=pltpu.CompilerParams(collective_id=0, has_side_effects=True, vmem_limit_bytes=28 << 20),
        name="gather",
    )(*args)


def score_kernel(qall, pbuf, lists, ranks, owners, acc, total, table, sem):
    qcount, qtok, dim = qall.shape
    pcount, plen, _ = pbuf.shape
    first = EARLY * LANES + UNROLL
    first = (first + LANES - 1) // LANES * LANES
    move = pltpu.make_async_copy(lists.at[:, :first], table.at[:, :first], sem)
    move.start()
    move.wait()

    @pl.when(table[9 + len(BOUNDS), 0] + UNROLL > first)
    def _():
        rest = pltpu.make_async_copy(lists.at[:, first:], table.at[:, first:], sem)
        rest.start()
        rest.wait()

    start = 0
    for c, rows in enumerate(BOUNDS + (plen,)):
        end = table[9 + c, 0]
        down = lax.broadcasted_iota(I32, (rows, 1), 0)

        def step(i, _, start=start, rows=rows, down=down):
            for u in range(UNROLL):
                b = start + i * UNROLL + u
                tokens = jnp.concatenate([qall[table[k, b]] for k in range(8)], axis=0)
                similar = nt(pbuf[table[8, b], :rows], tokens)
                similar = jnp.where(down < table[13, b], similar, -1e30)
                acc[pl.ds(b, 1), :] = jnp.max(similar, axis=0, keepdims=True)
            return 0

        whole = (end - start + (UNROLL - 1 if rows == plen else 0)) // UNROLL
        lax.fori_loop(0, whole, step, 0)
        start = start + whole * UNROLL
    total[...] = jnp.zeros_like(total)

    def late(j, _):
        spread(j, acc, ranks, owners, total, qtok)
        return 0

    lax.fori_loop(EARLY, (table[9 + len(BOUNDS), 0] + LANES - 1) // LANES, late, 0)


def spread(j, acc, ranks, owners, total, qtok):
    token = lax.broadcasted_iota(I32, (8, 8 * qtok), 1)
    mean = jnp.where(token // qtok == lax.broadcasted_iota(I32, (8, 8 * qtok), 0), 1.0 / qtok, 0.0).astype(BF16)
    best = acc[pl.ds(pl.multiple_of(j * LANES, LANES), LANES), :]
    high = best.astype(BF16)
    scores = nt(mean, high) + nt(mean, (best - high.astype(F32)).astype(BF16))
    seen = ranks[j]
    dense = sum(jnp.where(seen == float(k), scores[k : k + 1], 0.0) for k in range(8))
    high = dense.astype(BF16)
    both = jnp.concatenate([high, (dense - high.astype(F32)).astype(BF16)], axis=1)
    total[...] += nt(both, jnp.concatenate([owners[j]] * 2, axis=1))


def score(every, passages, lists, ranks, owners):
    qcount, qtok, _ = every.shape
    pcount = passages.shape[0]
    slots = lists.shape[1]
    vmem = pl.BlockSpec(memory_space=pltpu.VMEM)
    return pl.pallas_call(
        score_kernel,
        out_shape=(
            jax.ShapeDtypeStruct((slots, 8 * qtok), F32),
            jax.ShapeDtypeStruct((qcount, pcount), F32),
        ),
        in_specs=[vmem] * 5,
        out_specs=(vmem, vmem),
        scratch_shapes=[
            pltpu.SMEM((16, slots), I32),
            pltpu.SemaphoreType.DMA,
        ],
        compiler_params=pltpu.CompilerParams(vmem_limit_bytes=20 << 20),
        name="score",
    )(every, passages, lists, ranks, owners)


def return_kernel(
    count, acc, partial, ranks, owners, pairs_q, pairs_p, cand_ref, spots, out, total, compact, slabs, send, recv
):
    me = lax.axis_index("shard")
    block, ids = cand_ref.shape
    arrive = meet(me, count)
    total[...] = partial[...]
    for j in range(EARLY):
        spread(j, acc, ranks, owners, total, acc.shape[1] // 8)

    def pack(i, _):
        rows = total[pl.ds(pl.multiple_of(i * block, block), block), :]
        high = rows.astype(BF16)
        both = jnp.concatenate([high, (rows - high.astype(F32)).astype(BF16)], axis=0)
        found = jnp.dot(both, pairs_p[i], preferred_element_type=F32)
        found = (found[:block] + found[block:]) * pairs_q[i].astype(F32)
        compact[i] = jnp.sum(found, axis=0, keepdims=True)
        return 0

    lax.fori_loop(0, count, pack, 0, unroll=8)
    owner, _ = place_of(cand_ref[...], partial.shape[1])
    spot = spots[...]
    spot_w = jnp.concatenate([spot % LANES] * (LANES // ids), axis=1)
    arrive()

    def slab_copy(k):
        peer = (me + k) % count
        return pltpu.make_async_remote_copy(
            src_ref=compact.at[peer],
            dst_ref=slabs.at[me],
            send_sem=send.at[k],
            recv_sem=recv.at[k],
            device_id={"shard": peer},
            device_id_type=MESH,
        )

    def each(action):
        def go(k, _):
            action(slab_copy(k))
            return 0

        lax.fori_loop(1, count, go, 0, unroll=True)

    each(lambda copy: copy.start())
    slabs[me] = compact[me]
    each(lambda copy: copy.wait())
    result = jnp.zeros((block, ids), F32)
    for o in range(count):
        for part in range(ROOM // LANES):
            row = jnp.broadcast_to(slabs[o, :, part * LANES : (part + 1) * LANES], (block, LANES))
            found = jnp.take_along_axis(row, spot_w, axis=1)[:, :ids]
            result = jnp.where(jnp.logical_and(owner == o, spot // LANES == part), found, result)
    out[...] = result


def give_back(acc, partial, ranks, owners, pairs_q, pairs_p, candidates, spots):
    block, ids = candidates.shape
    count = pairs_q.shape[0]
    vmem = pl.BlockSpec(memory_space=pltpu.VMEM)
    dma = pltpu.SemaphoreType.DMA
    return pl.pallas_call(
        functools.partial(return_kernel, count),
        out_shape=jax.ShapeDtypeStruct((block, ids), F32),
        in_specs=[vmem] * 8,
        out_specs=vmem,
        scratch_shapes=[
            pltpu.VMEM(partial.shape, F32),
            pltpu.VMEM((count, 1, ROOM), F32),
            pltpu.VMEM((count, 1, ROOM), F32),
            dma((count,)),
            dma((count,)),
        ],
        compiler_params=pltpu.CompilerParams(collective_id=1, has_side_effects=True, vmem_limit_bytes=8 << 20),
        name="give_back",
    )(acc, partial, ranks, owners, pairs_q, pairs_p, candidates, spots)


def shards(queries, passages, lengths, candidates):
    count = lax.axis_size("shard")
    tokens_first = jnp.swapaxes(passages, 0, 1)
    every, kept, lists, ranks, owners, pairs_q, pairs_p, spots = gather(
        queries, candidates, tokens_first, lengths.reshape(1, -1), count
    )
    best, partial = score(every, kept, lists, ranks, owners)
    return give_back(best, partial, ranks, owners, pairs_q, pairs_p, candidates, spots)


def solution(mesh):
    in_specs = (
        P(("group", "shard"), None, None),
        P("shard", None, None),
        P("shard"),
        P(("group", "shard"), None),
    )
    out_specs = P(("group", "shard"), None)
    return jax.shard_map(shards, mesh=mesh, in_specs=in_specs, out_specs=out_specs, check_vma=False)
```
